512 devices in a mesh: grp: 16 (over y_hi, x, core), env: 32 (over z, y_lo).
Axes of the slice: x: 4, y: 8 (y_hi: 2, y_lo: 4; y = y_hi * 4 + y_lo), z: 8, core: 2. Of those that a mesh axis runs over, the one named last changes fastest.
Arguments:
- wavefunction: bfloat16 [8192, 4096], P('grp', 'env'), may hold values from -6 to 6
- left_tiles: bfloat16 [8192, 128, 128], P(('grp', 'env')), may hold values from -0.5 to 0.5
- right_tiles: bfloat16 [26, 4096, 128], P(None, 'env'), may hold values from -0.5 to 0.5
- term_source: int32 [8192], P('grp'), may hold values from 0 to 63
- term_target: int32 [8192], P('grp'), may hold values from 0 to 63
- right_index: int32 [8192], P('grp'), may hold values from 0 to 25
- term_sector: int32 [8192, 1], P('grp'), may hold values from 0 to 31; in each aligned block of 16 rows (0 to 15, 16 to 31, ...) at most 4 rows name the same one
- column_sector: int32 [32], replicated, may hold values from 0 to 31
Outputs:
- applied: bfloat16 [8192, 4096], P('grp', 'env')
The draws below stay inside these ranges and needn't reach their ends.
Inputs may be any that keep to these rules, and one draw needn't show every extreme that they name: `term_sector`: within each aligned block of 16 terms (the terms of one device) no sector appears more than 4 times, and every sector appears somewhere.
All inputs are finite; a program needn't handle non-finite values.
Results may differ from the reference program's by a relative error of at most 0.009.
Values may be sent and summed in bfloat16 or wider, within the bound.
No kernel may reach another device: no remote copies, remote signals or barrier semaphores. Data moves between devices by JAX's collectives and lax.ppermute only.
A program may use at most 64 MiB of HBM per device.

```python
import math
import jax
import jax.numpy as jnp
import numpy as np
from jax import lax

BLK = 128
NBLK = 64
NSEC = 32
NW = 26
MAXS = 4
TILES_DEV = 16
TG = 512
TERMS = 8192
ROWS = 8192
COLS = 4096
SLOTS = 128
N_GRP = 16
N_ENV = 32


def set_ends(drawn, own_key, smallest, high):
    shape = drawn.shape
    place = [jax.random.randint(jax.random.fold_in(own_key, axis), (), 0, shape[axis]) for axis in range(len(shape))]
    drawn = drawn.at[tuple(place)].set(smallest)
    longest = shape.index(max(shape))
    place[longest] = (place[longest] + 1) % shape[longest]
    return drawn.at[tuple(place)].set(high)


def shard_levels(key, dims, cuts, smallest, high):
    gain, own = 1.0, jax.random.fold_in(key, 6)
    for position, parts in cuts:
        heights = jnp.exp(jax.random.uniform(jax.random.fold_in(own, position), (parts,), jnp.float32, smallest / len(cuts), high / len(cuts)))
        gain = gain * jnp.repeat(heights, dims[position] // parts).reshape([-1 if axis == position else 1 for axis in range(len(dims))])
    return gain


def assign_block(rng, own, number, rows, count, top, limit, lean):
    sequence = jax.random.permutation(rng, count)
    packed, common = load_shares(count, rows * top, limit, lean, True), load_shares(count, rows * top, limit, lean, False)
    places = jnp.arange(count)

    def named(tallies, turn):
        used = int((tallies > 0).sum())
        fixed = max(1, used // 4)
        passed = fixed + (places - fixed + turn * (used - fixed)) % max(1, count - fixed)
        return jnp.zeros((count,), jnp.int32).at[sequence[jnp.where(places < fixed, places, passed)]].set(jnp.asarray(tallies, jnp.int32))

    tallies = jnp.where(number % 4 == 0, named(packed, number // 4), named(common, number - number // 4 - 1))
    mixed = jax.random.permutation(jax.random.fold_in(own, 3), count)
    source_of, receiver = mixed[0:count // 2 * 2:2], mixed[1:count // 2 * 2:2]
    room = jnp.minimum(tallies[source_of] - 1, limit - tallies[receiver]) // 2
    room = jnp.where((source_of == sequence[0]) | (receiver == sequence[0]) | (tallies[receiver] == 0), 0, jnp.maximum(room, 0))
    passed = jax.random.randint(jax.random.fold_in(own, 4), (count // 2,), 0, 1 << 20) % (room + 1)
    tallies = tallies.at[source_of].add(-passed).at[receiver].add(passed)
    labels = jnp.searchsorted(jnp.cumsum(tallies), jnp.arange(rows * top), side="right").astype(jnp.int32)
    listing = labels.reshape(top, rows).T
    listing = listing[jax.random.permutation(jax.random.fold_in(own, 1), rows)]
    turn = jax.random.randint(jax.random.fold_in(own, 2), (rows, 1), 0, top)
    return jnp.take_along_axis(listing, (jnp.arange(top)[None, :] + turn) % top, axis=1)


def load_shares(count, total, most, skew, full):
    weights = [(1 << 20) // math.isqrt(standing ** skew) + 1 for standing in range(1, count + 1)]
    largest = most if full else min(most, max(-(-total // count), total * weights[0] // sum(weights)))
    least = 1 if total - largest >= count - 1 else 0
    holding, rest = [largest] + [least] * (count - 1), total - largest - least * (count - 1)
    while rest > 0:
        free = [i for i in range(1, count) if holding[i] < largest] or [i for i in range(1, count) if holding[i] < most]
        whole, left = sum([weights[i] for i in free]), rest
        for i in free:
            more = min(most - holding[i], max(1, left * weights[i] // whole), rest)
            holding[i] = holding[i] + more
            rest = rest - more
    return np.array(holding)


def centred(stream_key, shape, scale, most, split=(), held_as=jnp.bfloat16):
    level = shard_levels(stream_key, shape, split, -0.22, 0.18) if split else 1.0
    drawn = jax.random.normal(stream_key, shape, jnp.float32) * scale * level
    return jnp.minimum(jnp.maximum(drawn, -most), most).astype(held_as)


def setup_inputs(seed: int = 0) -> dict:
    key_list = jax.random.split(jax.random.key(seed), 9)
    wavefunction = centred(key_list[0], (ROWS, COLS), 1.0, 6.0, ((0, 16), (1, 32)))
    left_tiles = centred(key_list[1], (TERMS, BLK, BLK), BLK ** -0.5, 0.5, ((0, 512),))
    right_tiles = centred(key_list[2], (NW, COLS, BLK), BLK ** -0.5, 0.5, ((1, 32),))
    term_source = set_ends(jax.random.randint(key_list[3], (TERMS,), 0, NBLK), jax.random.fold_in(key_list[3], 1), 0, NBLK - 1).astype(jnp.int32)
    term_target = set_ends(jax.random.randint(key_list[4], (TERMS,), 0, NBLK), jax.random.fold_in(key_list[4], 1), 0, NBLK - 1).astype(jnp.int32)
    right_index = set_ends(jax.random.randint(key_list[5], (TERMS,), 0, NW), jax.random.fold_in(key_list[5], 1), 0, NW - 1).astype(jnp.int32)
    term_sector_keys = jax.random.split(jax.random.fold_in(key_list[6], 1), TERMS // TILES_DEV)
    term_sector_turns = jax.random.permutation(jax.random.fold_in(key_list[6], 3), TERMS // TILES_DEV)
    term_sector = jax.vmap(lambda own, number: assign_block(jax.random.fold_in(key_list[6], 2), own, number, TILES_DEV, NSEC, 1, MAXS, 2))(term_sector_keys, term_sector_turns).reshape((TERMS, 1))
    column_sector = set_ends(jax.random.randint(key_list[7], (N_ENV,), 0, NSEC), jax.random.fold_in(key_list[7], 1), 0, NSEC - 1).astype(jnp.int32)
    return {"wavefunction": wavefunction, "left_tiles": left_tiles, "right_tiles": right_tiles, "term_source": term_source, "term_target": term_target, "right_index": right_index, "term_sector": term_sector, "column_sector": column_sector}


def group_part(left_group, source_group, target_group, right_group, sector_group, wavefunction, right_tiles, column_sector):
    def one_column(column):
        wanted = column_sector[column]
        missing = (sector_group != wanted).astype(jnp.int32)
        ordering = jnp.argsort(missing, stable=True)[:SLOTS]
        kept_mask = (1 - missing[ordering]).astype(jnp.float32)
        columns = lax.dynamic_slice_in_dim(wavefunction, column * BLK, BLK, 1).reshape(NBLK, BLK, BLK)
        right_cols = lax.dynamic_slice_in_dim(right_tiles, column * BLK, BLK, 1)
        left_pick = left_group[ordering].astype(jnp.float32)
        source_blocks = columns[source_group[ordering]].astype(jnp.float32)
        block_product = jnp.einsum("kab,kbc->kac", left_pick, source_blocks, precision=lax.Precision.HIGHEST).astype(jnp.bfloat16)
        block_product = lax.optimization_barrier(block_product).astype(jnp.float32)
        right_pick = right_cols[right_group[ordering]].astype(jnp.float32)
        term_image = jnp.einsum("kac,kcd->kad", block_product, right_pick, precision=lax.Precision.HIGHEST)
        term_image = term_image * kept_mask[:, None, None]
        summed_rows = jnp.zeros((NBLK, BLK, BLK), jnp.float32).at[target_group[ordering]].add(term_image)
        return summed_rows.reshape(ROWS, BLK)

    pieces = lax.map(one_column, jnp.arange(N_ENV, dtype=jnp.int32))
    return jnp.transpose(pieces, (1, 0, 2)).reshape(ROWS, COLS).astype(jnp.bfloat16)


def reference(wavefunction, left_tiles, right_tiles, term_source, term_target, right_index, term_sector, column_sector):
    sectors = term_sector[:, 0]

    def one_group(running, group):
        first_term = group * TG

        def take_group(values):
            return lax.dynamic_slice_in_dim(values, first_term, TG, 0)

        group_partial = group_part(take_group(left_tiles), take_group(term_source), take_group(term_target), take_group(right_index), take_group(sectors), wavefunction, right_tiles, column_sector)
        return running + group_partial.astype(jnp.float32), None

    summed, ignored_out = lax.scan(one_group, jnp.zeros((ROWS, COLS), jnp.float32), jnp.arange(N_GRP, dtype=jnp.int32))
    return summed.astype(jnp.bfloat16)
```

```python
import jax
import jax.numpy as jnp
from jax import lax
from jax.experimental import pallas as pl
from jax.experimental.pallas import tpu as pltpu
from jax.sharding import PartitionSpec as P

SLOTS = 4
UNROLL = 4


def pack_kernel(per, sector, column, tiles, out, heads, nexts, counts):
    place = lax.axis_index("env")
    columns = column.shape[0]
    sectors = heads.shape[0]

    def clear(s, carry):
        heads[s] = -1
        counts[s] = 0
        return carry

    lax.fori_loop(0, sectors, clear, 0)

    def chain(c, carry):
        s = column[c]
        nexts[c] = heads[s]
        heads[s] = c
        return carry

    lax.fori_loop(0, columns, chain, 0)

    def tile(i, carry):
        s = sector[place * per + i]
        k = counts[s]
        counts[s] = k + 1

        def send(c):
            out[c * SLOTS + k] = tiles[i]
            return nexts[c]

        lax.while_loop(lambda c: c >= 0, send, heads[s])
        return carry

    lax.fori_loop(0, per, tile, 0)


def apply_kernel(
    per, sector, source, target, index, column, tiles, blocks, rights, out, picked, acc
):
    wanted = column[lax.axis_index("env")]
    groups = sector.shape[0] // per

    def scan(b, n):
        k = jnp.int32(0)
        for i in range(per):
            t = b * per + i
            match = (sector[t] == wanted).astype(jnp.int32)
            picked[n] = t * SLOTS + k
            n = n + match
            k = k + match
        return n

    n = lax.fori_loop(0, groups, scan, jnp.int32(0))
    for j in range(UNROLL):
        picked[n + j] = -1
    count = out.shape[0]

    def clear(r, carry):
        acc[r] = jnp.zeros(acc.shape[1:], acc.dtype)
        return carry

    lax.fori_loop(0, count, clear, 0)

    def terms(j, carry):
        for u in range(UNROLL):
            entry = picked[j * UNROLL + u]
            kept = jnp.maximum(entry, 0)
            t = kept // SLOTS
            slot = (t // per) * SLOTS + kept % SLOTS
            row = jnp.where(entry < 0, count, target[t])
            product = jnp.dot(
                tiles[slot], blocks[source[t]], preferred_element_type=jnp.float32
            ).astype(jnp.bfloat16)
            acc[row] += jnp.dot(
                product, rights[index[t]], preferred_element_type=jnp.float32
            )
        return carry

    lax.fori_loop(0, (n + UNROLL - 1) // UNROLL, terms, 0)

    def finish(r, carry):
        out[r] = acc[r].astype(out.dtype)
        return carry

    lax.fori_loop(0, count, finish, 0)


def shards(
    wavefunction,
    left_tiles,
    right_tiles,
    term_source,
    term_target,
    right_index,
    term_sector,
    column_sector,
):
    per, size, _ = left_tiles.shape
    columns = column_sector.shape[0]
    slots = columns * SLOTS
    smem = pl.BlockSpec(memory_space=pltpu.SMEM)
    vmem = pl.BlockSpec(memory_space=pltpu.VMEM)
    sectors = term_sector[:, 0]
    blocks = lax.all_gather(wavefunction, "grp", axis=0, tiled=True)
    count = blocks.shape[0] // size
    blocks = blocks.reshape(count, size, size)
    packed = pl.pallas_call(
        lambda *refs: pack_kernel(per, *refs),
        out_shape=jax.ShapeDtypeStruct((slots, size, size), jnp.bfloat16),
        in_specs=[smem, smem, vmem],
        out_specs=vmem,
        scratch_shapes=[
            pltpu.SMEM((columns,), jnp.int32),
            pltpu.SMEM((columns,), jnp.int32),
            pltpu.SMEM((columns,), jnp.int32),
        ],
        compiler_params=pltpu.CompilerParams(vmem_limit_bytes=16 * 2**20),
    )(sectors, column_sector, left_tiles)
    tiles = lax.all_to_all(packed, "env", 0, 0, tiled=True)
    partial = pl.pallas_call(
        lambda *refs: apply_kernel(per, *refs),
        out_shape=jax.ShapeDtypeStruct((count, size, size), jnp.bfloat16),
        in_specs=[smem] * 5 + [vmem] * 3,
        out_specs=vmem,
        scratch_shapes=[
            pltpu.SMEM((sectors.shape[0] + UNROLL,), jnp.int32),
            pltpu.VMEM((count + 1, size, size), jnp.float32),
        ],
        compiler_params=pltpu.CompilerParams(vmem_limit_bytes=32 * 2**20),
    )(
        sectors,
        term_source,
        term_target,
        right_index,
        column_sector,
        tiles,
        blocks,
        right_tiles,
    )
    parts = lax.all_to_all(partial, "grp", 0, 0, tiled=True)
    groups = lax.axis_size("grp")
    parts = parts.reshape(groups, -1, size)
    return jnp.sum(parts.astype(jnp.float32), axis=0).astype(jnp.bfloat16)


def solution(mesh):
    placed = (
        P("grp", "env"),
        P(("grp", "env"), None, None),
        P(None, "env", None),
        P("grp"),
        P("grp"),
        P("grp"),
        P("grp", None),
        P(),
    )
    return jax.shard_map(
        shards, mesh=mesh, in_specs=placed, out_specs=P("grp", "env"), check_vma=False
    )
```

```python
import jax
import jax.numpy as jnp
from jax import lax
from jax.experimental import pallas as pl
from jax.experimental.pallas import tpu as pltpu
from jax.sharding import Mesh
from jax.sharding import PartitionSpec as P

GRP = ("y_hi", "x", "core")
ENV = ("z", "y_lo")
HALVES, XS, CORES = 2, 4, 2
DEEP, LOW = 8, 4
ROWS_DEV = 4
SLOTS = 4
UNROLL = 4


def env_place():
    return lax.axis_index("z") * lax.axis_size("y_lo") + lax.axis_index("y_lo")


def pack_kernel(per, sector, column, tiles, out, heads, nexts, counts):
    place = env_place()
    columns = column.shape[0]
    sectors = heads.shape[0]

    def clear(s, carry):
        heads[s] = -1
        counts[s] = 0
        return carry

    lax.fori_loop(0, sectors, clear, 0)

    def chain(c, carry):
        s = column[c]
        nexts[c] = heads[s]
        heads[s] = c
        return carry

    lax.fori_loop(0, columns, chain, 0)

    def tile(i, carry):
        s = sector[place * per + i]
        k = counts[s]
        counts[s] = k + 1

        def send(c):
            out[c * SLOTS + k] = tiles[i]
            return nexts[c]

        lax.while_loop(lambda c: c >= 0, send, heads[s])
        return carry

    lax.fori_loop(0, per, tile, 0)


def place_of(row, core):
    group = row // ROWS_DEV
    rest = row % ROWS_DEV
    other = (group % CORES) ^ core
    return ((other * XS + (group // CORES) % XS) * HALVES + group // (CORES * XS)) * ROWS_DEV + rest


def apply_kernel(
    per, sector, source, target, index, column, tiles, near, far, rights, mine, theirs, picked, acc, blocks
):
    wanted = column[env_place()]
    core = lax.axis_index("core")
    half = near.shape[0]
    count = 2 * half

    def gather(r, carry):
        blocks[r] = near[r]
        blocks[half + r] = far[r]
        return carry

    lax.fori_loop(0, half, gather, 0)
    groups = sector.shape[0] // per

    def scan(b, n):
        k = jnp.int32(0)
        for i in range(per):
            t = b * per + i
            match = (sector[t] == wanted).astype(jnp.int32)
            picked[n] = t * SLOTS + k
            n = n + match
            k = k + match
        return n

    n = lax.fori_loop(0, groups, scan, jnp.int32(0))
    for j in range(UNROLL):
        picked[n + j] = -1

    def clear(r, carry):
        acc[r] = jnp.zeros(acc.shape[1:], acc.dtype)
        return carry

    lax.fori_loop(0, count, clear, 0)

    def terms(j, carry):
        for u in range(UNROLL):
            entry = picked[j * UNROLL + u]
            kept = jnp.maximum(entry, 0)
            t = kept // SLOTS
            slot = (t // per) * SLOTS + kept % SLOTS
            row = jnp.where(entry < 0, count, place_of(target[t], core))
            product = jnp.dot(
                tiles[slot], blocks[place_of(source[t], core)], preferred_element_type=jnp.float32
            ).astype(jnp.bfloat16)
            acc[row] += jnp.dot(
                product, rights[index[t]], preferred_element_type=jnp.float32
            )
        return carry

    lax.fori_loop(0, (n + UNROLL - 1) // UNROLL, terms, 0)

    def finish(r, carry):
        mine[r] = acc[r].astype(mine.dtype)
        theirs[r] = acc[half + r].astype(theirs.dtype)
        return carry

    lax.fori_loop(0, half, finish, 0)


def shards(
    wavefunction,
    left_tiles,
    right_tiles,
    term_source,
    term_target,
    right_index,
    term_sector,
    column_sector,
):
    per, size, _ = left_tiles.shape
    columns = column_sector.shape[0]
    slots = columns * SLOTS
    smem = pl.BlockSpec(memory_space=pltpu.SMEM)
    vmem = pl.BlockSpec(memory_space=pltpu.VMEM)
    sectors = term_sector[:, 0]
    psi = wavefunction.reshape(-1, size, size)
    near = lax.all_gather(psi, "y_hi", axis=0, tiled=True)
    near = lax.all_gather(near, "x", axis=0, tiled=True)
    swap = [(0, 1), (1, 0)]
    far = lax.ppermute(near, "core", swap)
    half = near.shape[0]
    packed = pl.pallas_call(
        lambda *refs: pack_kernel(per, *refs),
        out_shape=jax.ShapeDtypeStruct((slots, size, size), jnp.bfloat16),
        in_specs=[smem, smem, vmem],
        out_specs=vmem,
        scratch_shapes=[
            pltpu.SMEM((columns,), jnp.int32),
            pltpu.SMEM((columns,), jnp.int32),
            pltpu.SMEM((columns,), jnp.int32),
        ],
        compiler_params=pltpu.CompilerParams(vmem_limit_bytes=16 * 2**20),
    )(sectors, column_sector, left_tiles)
    tiles = lax.all_to_all(packed, ENV, 0, 0, tiled=True)
    block = jax.ShapeDtypeStruct((half, size, size), jnp.bfloat16)
    mine, theirs = pl.pallas_call(
        lambda *refs: apply_kernel(per, *refs),
        out_shape=(block, block),
        in_specs=[smem] * 5 + [vmem] * 4,
        out_specs=(vmem, vmem),
        scratch_shapes=[
            pltpu.SMEM((sectors.shape[0] + UNROLL,), jnp.int32),
            pltpu.VMEM((2 * half + 1, size, size), jnp.float32),
            pltpu.VMEM((2 * half, size, size), jnp.bfloat16),
        ],
        compiler_params=pltpu.CompilerParams(vmem_limit_bytes=40 * 2**20),
    )(
        sectors,
        term_source,
        term_target,
        right_index,
        column_sector,
        tiles,
        near,
        far,
        right_tiles,
    )
    total = mine.astype(jnp.float32) + lax.ppermute(theirs, "core", swap).astype(
        jnp.float32
    )
    for axis in ("x", "y_hi"):
        parts = lax.all_to_all(total.astype(jnp.bfloat16), axis, 0, 0, tiled=True)
        parts = parts.reshape((lax.axis_size(axis), -1) + parts.shape[1:])
        total = jnp.sum(parts.astype(jnp.float32), axis=0)
    return total.astype(jnp.bfloat16).reshape(wavefunction.shape)


def solution(mesh):
    physical = Mesh(
        mesh.devices.reshape(HALVES, XS, CORES, DEEP, LOW), GRP + ENV
    )
    placed = (
        P(GRP, ENV),
        P(GRP + ENV, None, None),
        P(None, ENV, None),
        P(GRP),
        P(GRP),
        P(GRP),
        P(GRP, None),
        P(),
    )
    return jax.shard_map(
        shards, mesh=physical, in_specs=placed, out_specs=P(GRP, ENV), check_vma=False
    )
```

```python
import jax
import jax.numpy as jnp
from jax import lax
from jax.experimental import pallas as pl
from jax.experimental.pallas import tpu as pltpu
from jax.sharding import Mesh
from jax.sharding import PartitionSpec as P

GRP = ("y_hi", "x", "core")
ENV = ("z", "y_lo")
HALVES, XS, CORES = 2, 4, 2
DEEP, LOW = 8, 4
ROWS_DEV = 4
SLOTS = 4
UNROLL = 4
LANES = 128


def env_place():
    return lax.axis_index("z") * LOW + lax.axis_index("y_lo")


def pack_kernel(per, sector, column, sector_rows, tiles, out, need, heads, nexts, counts):
    place = env_place()
    columns = column.shape[0]
    sectors = heads.shape[0]

    rows = sector_rows[...]
    lane = lax.broadcasted_iota(jnp.int32, rows.shape, 1) % per
    rank = jnp.ones(rows.shape, jnp.int32)
    for step in range(1, per):
        same = (pltpu.roll(rows, step, 1) == rows) & (lane >= step)
        rank = rank + same.astype(jnp.int32)
    wanted = rows == column[0]
    for c in range(1, columns):
        wanted = wanted | (rows == column[c])
    slots = jnp.maximum(jnp.max(jnp.where(wanted, rank, 0)), 1)
    need[0] = slots

    def clear(s, carry):
        heads[s] = -1
        counts[s] = 0
        return carry

    lax.fori_loop(0, sectors, clear, 0)

    def chain(c, carry):
        s = column[c]
        nexts[c] = heads[s]
        heads[s] = c
        return carry

    lax.fori_loop(0, columns, chain, 0)

    def tile(i, carry):
        s = sector[place * per + i]
        k = counts[s]
        counts[s] = k + 1

        def send(c):
            out[c * slots + k] = tiles[i]
            return nexts[c]

        lax.while_loop(lambda c: c >= 0, send, heads[s])
        return carry

    lax.fori_loop(0, per, tile, 0)


def apply_kernel(
    per,
    sector,
    source,
    target,
    index,
    column,
    need,
    tiles,
    near,
    far,
    rights,
    mine,
    theirs,
    picked,
    acc,
    blocks,
):
    wanted = column[env_place()]
    slots = need[0]
    half_at, x_at, core_at = (lax.axis_index(a) for a in GRP)
    groups = sector.shape[0] // per
    half = near.shape[0]
    count = 2 * half

    def read_place(row):
        group = row // ROWS_DEV
        core = (group % CORES) ^ core_at
        x = (x_at - (group // CORES) % XS) % XS
        y = group // (CORES * XS) ^ half_at
        return ((core * XS + x) * HALVES + y) * ROWS_DEV + row % ROWS_DEV

    def write_place(row):
        group = row // ROWS_DEV
        core = (group % CORES) ^ core_at
        x = (group // CORES) % XS
        y = group // (CORES * XS)
        return ((core * XS + x) * HALVES + y) * ROWS_DEV + row % ROWS_DEV

    def fill(r, carry):
        blocks[r] = near[r]
        blocks[half + r] = far[r]
        acc[r] = jnp.zeros(acc.shape[1:], acc.dtype)
        acc[half + r] = jnp.zeros(acc.shape[1:], acc.dtype)
        return carry

    lax.fori_loop(0, half, fill, 0)

    def scan(b, n):
        k = jnp.int32(0)
        for i in range(per):
            t = b * per + i
            match = (sector[t] == wanted).astype(jnp.int32)
            picked[n] = t * SLOTS + k
            n = n + match
            k = k + match
        return n

    n = lax.fori_loop(0, groups, scan, jnp.int32(0))
    for j in range(UNROLL):
        picked[n + j] = -1

    def terms(j, carry):
        for u in range(UNROLL):
            entry = picked[j * UNROLL + u]
            kept = jnp.maximum(entry, 0)
            t = kept // SLOTS
            slot = (t // per) * slots + kept % SLOTS
            row = jnp.where(entry < 0, count, write_place(target[t]))
            product = jnp.dot(
                tiles[slot],
                blocks[read_place(source[t])],
                preferred_element_type=jnp.float32,
            ).astype(jnp.bfloat16)
            acc[row] += jnp.dot(
                product, rights[index[t]], preferred_element_type=jnp.float32
            )
        return carry

    lax.fori_loop(0, (n + UNROLL - 1) // UNROLL, terms, 0)

    def finish(r, carry):
        mine[r] = acc[r].astype(mine.dtype)
        theirs[r] = acc[half + r].astype(theirs.dtype)
        return carry

    lax.fori_loop(0, half, finish, 0)


def swap(value, axis):
    return lax.ppermute(value, axis, [(0, 1), (1, 0)])


def step_x(value, step):
    return lax.ppermute(value, "x", [(i, (i + step) % XS) for i in range(XS)])


def exchange(slots):
    def run(packed):
        got = lax.all_to_all(packed[: DEEP * LOW * slots], ENV, 0, 0, tiled=True)
        if slots == SLOTS:
            return got
        rest = jnp.zeros((packed.shape[0] - got.shape[0],) + got.shape[1:], got.dtype)
        return jnp.concatenate([got, rest])

    return run


def shards(
    wavefunction,
    left_tiles,
    right_tiles,
    term_source,
    term_target,
    right_index,
    term_sector,
    column_sector,
):
    per, size, _ = left_tiles.shape
    columns = column_sector.shape[0]
    smem = pl.BlockSpec(memory_space=pltpu.SMEM)
    vmem = pl.BlockSpec(memory_space=pltpu.VMEM)
    sectors = term_sector[:, 0]

    psi = wavefunction.reshape(-1, size, size)
    pair = jnp.concatenate([psi, swap(psi, "y_hi")])
    packed, need = pl.pallas_call(
        lambda *refs: pack_kernel(per, *refs),
        out_shape=(
            jax.ShapeDtypeStruct((columns * SLOTS, size, size), jnp.bfloat16),
            jax.ShapeDtypeStruct((1,), jnp.int32),
        ),
        in_specs=[smem, smem, vmem, vmem],
        out_specs=(vmem, smem),
        scratch_shapes=[pltpu.SMEM((columns,), jnp.int32)] * 3,
        compiler_params=pltpu.CompilerParams(vmem_limit_bytes=16 * 2**20),
        cost_estimate=pl.CostEstimate(
            flops=0, bytes_accessed=8 * 2**20, transcendentals=0
        ),
    )(sectors, column_sector, sectors.reshape(-1, LANES), left_tiles)
    packed, pair = lax.optimization_barrier((packed, pair))
    near = [pair] + [step_x(pair, step) for step in range(1, XS)]
    tiles = lax.switch(need[0] - 1, [exchange(k + 1) for k in range(SLOTS)], packed)
    tiles, near = lax.optimization_barrier((tiles, near))
    near = jnp.concatenate(near)
    far = swap(near, "core")
    half = near.shape[0]
    block = jax.ShapeDtypeStruct((half, size, size), jnp.bfloat16)
    mine, theirs = pl.pallas_call(
        lambda *refs: apply_kernel(per, *refs),
        out_shape=(block, block),
        in_specs=[smem] * 6 + [vmem] * 4,
        out_specs=(vmem, vmem),
        scratch_shapes=[
            pltpu.SMEM((sectors.shape[0] + UNROLL,), jnp.int32),
            pltpu.VMEM((2 * half + 1, size, size), jnp.float32),
            pltpu.VMEM((2 * half, size, size), jnp.bfloat16),
        ],
        compiler_params=pltpu.CompilerParams(vmem_limit_bytes=40 * 2**20),
    )(
        sectors,
        term_source,
        term_target,
        right_index,
        column_sector,
        need,
        tiles,
        near,
        far,
        right_tiles,
    )
    total = mine.astype(jnp.float32) + swap(theirs, "core").astype(jnp.float32)
    for axis in ("x", "y_hi"):
        parts = lax.all_to_all(total.astype(jnp.bfloat16), axis, 0, 0, tiled=True)
        parts = parts.reshape((lax.axis_size(axis), -1) + parts.shape[1:])
        total = jnp.sum(parts.astype(jnp.float32), axis=0)
    return total.astype(jnp.bfloat16).reshape(wavefunction.shape)


def solution(mesh):
    physical = Mesh(mesh.devices.reshape(HALVES, XS, CORES, DEEP, LOW), GRP + ENV)
    placed = (
        P(GRP, ENV),
        P(GRP + ENV, None, None),
        P(None, ENV, None),
        P(GRP),
        P(GRP),
        P(GRP),
        P(GRP, None),
        P(),
    )
    return jax.shard_map(
        shards, mesh=physical, in_specs=placed, out_specs=P(GRP, ENV), check_vma=False
    )
```

```python
import jax
import jax.numpy as jnp
from jax import lax
from jax.experimental import pallas as pl
from jax.experimental.pallas import tpu as pltpu
from jax.sharding import Mesh
from jax.sharding import PartitionSpec as P

GRP = ("y_hi", "x", "core")
ENV = ("z", "y_lo")
HALVES, XS, CORES = 2, 4, 2
DEEP, LOW = 8, 4
ROWS_DEV = 4
SLOTS = 4
UNROLL = 4
LANES = 128


def env_place():
    return lax.axis_index("z") * LOW + lax.axis_index("y_lo")


def pack_kernel(
    per,
    sector,
    column,
    sector_rows,
    tiles,
    out_1,
    out_2,
    out_3,
    out_4,
    need,
    picked,
    heads,
    nexts,
    counts,
    started,
    copies,
):
    place = env_place()
    columns = column.shape[0]
    sectors = heads.shape[0]

    rows = sector_rows[...]
    lane = lax.broadcasted_iota(jnp.int32, rows.shape, 1) % per
    rank = jnp.ones(rows.shape, jnp.int32)
    for step in range(1, per):
        same = (pltpu.roll(rows, step, 1) == rows) & (lane >= step)
        rank = rank + same.astype(jnp.int32)
    wanted = rows == column[0]
    for c in range(1, columns):
        wanted = wanted | (rows == column[c])
    slots = jnp.maximum(jnp.max(jnp.where(wanted, rank, 0)), 1)
    need[0] = slots

    def clear(s, carry):
        heads[s] = -1
        counts[s] = 0
        return carry

    lax.fori_loop(0, sectors, clear, 0, unroll=8)

    def chain(c, carry):
        s = column[c]
        nexts[c] = heads[s]
        heads[s] = c
        return carry

    lax.fori_loop(0, columns, chain, 0, unroll=8)

    outs = (out_1, out_2, out_3, out_4)

    def move(i, out, slot, place):
        return pltpu.make_async_copy(tiles.at[i], out.at[place], copies.at[slot])

    def tile(i, n):
        s = sector[place * per + i]
        k = counts[s]
        counts[s] = k + 1

        def send(state):
            c, n = state
            slot = c * slots + k
            for size in range(1, SLOTS + 1):

                @pl.when(slots == size)
                def _(size=size):
                    move(i, outs[size - 1], slot, slot).start()

            started[n] = slot
            return nexts[c], n + 1

        return lax.while_loop(lambda state: state[0] >= 0, send, (heads[s], n))[1]

    sent = lax.fori_loop(0, per, tile, jnp.int32(0))

    mine = column[place]

    def scan(b, n):
        k = b * slots
        for i in range(per):
            t = b * per + i
            match = (sector[t] == mine).astype(jnp.int32)
            picked[n] = t * LANES + k
            n = n + match
            k = k + match
        return n

    n = lax.fori_loop(0, sector.shape[0] // per, scan, jnp.int32(1))
    for j in range(UNROLL):
        picked[n + j] = -1
    picked[0] = n - 1

    def finish(j, carry):
        move(0, out_1, started[j], 0).wait()
        return carry

    lax.fori_loop(0, sent, finish, 0)


def apply_kernel(
    source,
    target,
    index,
    picked,
    tiles,
    part_0,
    part_1,
    part_2,
    part_3,
    rights,
    out_stay,
    out_cross,
    out_other_stay,
    out_other_cross,
    held,
    acc,
    blocks,
    copied,
):
    load = pltpu.make_async_copy(tiles, held, copied)
    load.start()
    half_at, x_at, core_at = (lax.axis_index(a) for a in GRP)
    quarter = out_stay.shape[0]
    count = 4 * quarter

    def read_place(row):
        group = row // ROWS_DEV
        core = (group % CORES) ^ core_at
        x = (x_at - (group // CORES) % XS + XS) % XS
        y = group // (CORES * XS) ^ half_at
        return ((x * CORES + core) * HALVES + y) * ROWS_DEV + row % ROWS_DEV

    def write_place(row):
        group = row // ROWS_DEV
        core = (group % CORES) ^ core_at
        x = (group // CORES) % XS
        y = group // (CORES * XS) ^ half_at
        return ((core * HALVES + y) * XS + x) * ROWS_DEV + row % ROWS_DEV

    parts = (part_0, part_1, part_2, part_3)
    part = part_0.shape[0]

    def fill(r, carry):
        for x in range(XS):
            blocks[x * part + r] = parts[x][r]
            acc[x * part + r] = jnp.zeros(acc.shape[1:], acc.dtype)
        return carry

    lax.fori_loop(0, part, fill, 0)
    load.wait()

    def terms(j, carry):
        for u in range(UNROLL):
            entry = picked[1 + j * UNROLL + u]
            kept = jnp.maximum(entry, 0)
            t = kept // LANES
            slot = kept % LANES
            row = jnp.where(entry < 0, count, write_place(target[t]))
            product = jnp.dot(
                held[slot],
                blocks[read_place(source[t])],
                preferred_element_type=jnp.float32,
            ).astype(jnp.bfloat16)
            acc[row] += jnp.dot(
                product, rights[index[t]], preferred_element_type=jnp.float32
            )
        return carry

    lax.fori_loop(0, (picked[0] + UNROLL - 1) // UNROLL, terms, 0)

    def finish(r, carry):
        for place, out in enumerate(
            (out_stay, out_cross, out_other_stay, out_other_cross)
        ):
            out[r] = acc[place * quarter + r].astype(out.dtype)
        return carry

    lax.fori_loop(0, quarter, finish, 0)


def place_kernel(got, out, copied):
    move = pltpu.make_async_copy(got, out.at[pl.ds(0, got.shape[0])], copied)
    move.start()
    move.wait()


def swap(value, axis):
    return lax.ppermute(value, axis, [(0, 1), (1, 0)])


def sum_x(own, got):
    total = own.astype(jnp.float32) + got.astype(jnp.float32)
    parts = lax.all_to_all(total.astype(jnp.bfloat16), "x", 0, 0, tiled=True)
    parts = parts.reshape((XS, -1) + parts.shape[1:])
    return jnp.sum(parts.astype(jnp.float32), axis=0)


def step_x(value, step):
    return lax.ppermute(value, "x", [(i, (i + step) % XS) for i in range(XS)])


def exchange(slots, packing):
    def run(*packed):
        got = lax.all_to_all(packed[slots - 1], ENV, 0, 0, tiled=True)
        if slots == SLOTS:
            return got
        return pl.pallas_call(
            place_kernel,
            out_shape=packing,
            in_specs=[pl.BlockSpec(memory_space=pltpu.VMEM)],
            out_specs=pl.BlockSpec(memory_space=pl.ANY),
            scratch_shapes=[pltpu.SemaphoreType.DMA],
        )(got)

    return run


def shards(
    wavefunction,
    left_tiles,
    right_tiles,
    term_source,
    term_target,
    right_index,
    term_sector,
    column_sector,
):
    per, size, _ = left_tiles.shape
    columns = column_sector.shape[0]
    smem = pl.BlockSpec(memory_space=pltpu.SMEM)
    vmem = pl.BlockSpec(memory_space=pltpu.VMEM)
    anywhere = pl.BlockSpec(memory_space=pl.ANY)
    sectors = term_sector[:, 0]
    slots = columns * SLOTS
    packing = jax.ShapeDtypeStruct((slots, size, size), jnp.bfloat16)

    psi = wavefunction.reshape(-1, size, size)
    pair = jnp.concatenate([psi, swap(psi, "y_hi")])
    *packed, need, picked = pl.pallas_call(
        lambda *refs: pack_kernel(per, *refs),
        out_shape=(
            *[
                jax.ShapeDtypeStruct((columns * (k + 1), size, size), jnp.bfloat16)
                for k in range(SLOTS)
            ],
            jax.ShapeDtypeStruct((1,), jnp.int32),
            jax.ShapeDtypeStruct((sectors.shape[0] + 1 + UNROLL,), jnp.int32),
        ),
        in_specs=[smem, smem, vmem, vmem],
        out_specs=(*[anywhere] * SLOTS, smem, smem),
        scratch_shapes=[pltpu.SMEM((columns,), jnp.int32)] * 3
        + [pltpu.SMEM((slots,), jnp.int32), pltpu.SemaphoreType.DMA((slots,))],
        cost_estimate=pl.CostEstimate(
            flops=0, bytes_accessed=8 * 2**20, transcendentals=0
        ),
    )(sectors, column_sector, sectors.reshape(-1, LANES), left_tiles)
    packed, pair = lax.optimization_barrier((packed, pair))
    quad = jnp.concatenate([pair, swap(pair, "core")])
    parts = [quad] + [step_x(quad, step) for step in range(1, XS)]
    tiles = lax.switch(
        need[0] - 1, [exchange(k + 1, packing) for k in range(SLOTS)], *packed
    )
    tiles, parts = lax.optimization_barrier((tiles, parts))
    quarter = quad.shape[0]
    block = jax.ShapeDtypeStruct(quad.shape, jnp.bfloat16)
    stay, cross, other_stay, other_cross = pl.pallas_call(
        apply_kernel,
        out_shape=[block] * 4,
        in_specs=[smem] * 4 + [anywhere] + [vmem] * 5,
        out_specs=[vmem] * 4,
        scratch_shapes=[
            pltpu.VMEM(packing.shape, jnp.bfloat16),
            pltpu.VMEM((4 * quarter + 1, size, size), jnp.float32),
            pltpu.VMEM((4 * quarter, size, size), jnp.bfloat16),
            pltpu.SemaphoreType.DMA,
        ],
        compiler_params=pltpu.CompilerParams(vmem_limit_bytes=40 * 2**20),
    )(
        term_source,
        term_target,
        right_index,
        picked,
        tiles,
        *parts,
        right_tiles,
    )
    cross = sum_x(cross, swap(other_cross, "core"))
    crossed = swap(cross.astype(jnp.bfloat16), "y_hi")
    stay = sum_x(stay, swap(other_stay, "core"))
    total = stay + crossed.astype(jnp.float32)
    return total.astype(jnp.bfloat16).reshape(wavefunction.shape)


def solution(mesh):
    physical = Mesh(mesh.devices.reshape(HALVES, XS, CORES, DEEP, LOW), GRP + ENV)
    placed = (
        P(GRP, ENV),
        P(GRP + ENV, None, None),
        P(None, ENV, None),
        P(GRP),
        P(GRP),
        P(GRP),
        P(GRP, None),
        P(),
    )
    return jax.shard_map(
        shards, mesh=physical, in_specs=placed, out_specs=P(GRP, ENV), check_vma=False
    )
```

```python
import jax
import jax.numpy as jnp
from jax import lax
from jax.experimental import pallas as pl
from jax.experimental.pallas import tpu as pltpu
from jax.sharding import Mesh
from jax.sharding import PartitionSpec as P

GRP = ("y_hi", "x", "core")
ENV = ("z", "y_lo")
HALVES, XS, CORES = 2, 4, 2
DEEP, LOW = 8, 4
ROWS_DEV = 4
SLOTS = 4
UNROLL = 4
LANES = 128


def env_place():
    return lax.axis_index("z") * LOW + lax.axis_index("y_lo")


def pack_kernel(
    per,
    sector,
    column,
    sector_rows,
    tiles,
    out_1,
    out_2,
    out_3,
    out_4,
    need,
    picked,
    heads,
    nexts,
    counts,
    started,
    copies,
):
    place = env_place()
    columns = column.shape[0]
    sectors = heads.shape[0]

    rows = sector_rows[...]
    lane = lax.broadcasted_iota(jnp.int32, rows.shape, 1) % per
    rank = jnp.ones(rows.shape, jnp.int32)
    for step in range(1, per):
        same = (pltpu.roll(rows, step, 1) == rows) & (lane >= step)
        rank = rank + same.astype(jnp.int32)
    wanted = rows == column[0]
    for c in range(1, columns):
        wanted = wanted | (rows == column[c])
    slots = jnp.maximum(jnp.max(jnp.where(wanted, rank, 0)), 1)
    need[0] = slots

    def clear(s, carry):
        heads[s] = -1
        counts[s] = 0
        return carry

    lax.fori_loop(0, sectors, clear, 0, unroll=8)

    def chain(c, carry):
        s = column[c]
        nexts[c] = heads[s]
        heads[s] = c
        return carry

    lax.fori_loop(0, columns, chain, 0, unroll=8)

    outs = (out_1, out_2, out_3, out_4)

    def move(i, out, slot, place):
        return pltpu.make_async_copy(tiles.at[i], out.at[place], copies.at[slot])

    def tile(i, n):
        s = sector[place * per + i]
        k = counts[s]
        counts[s] = k + 1

        def send(state):
            c, n = state
            slot = c * slots + k
            for size in range(1, SLOTS + 1):

                @pl.when(slots == size)
                def _(size=size):
                    move(i, outs[size - 1], slot, slot).start()

            started[n] = slot
            return nexts[c], n + 1

        return lax.while_loop(lambda state: state[0] >= 0, send, (heads[s], n))[1]

    sent = lax.fori_loop(0, per, tile, jnp.int32(0))

    mine = column[place]

    def scan(b, n):
        k = b * slots
        for i in range(per):
            t = b * per + i
            match = (sector[t] == mine).astype(jnp.int32)
            picked[n] = t * LANES + k
            n = n + match
            k = k + match
        return n

    n = lax.fori_loop(0, sector.shape[0] // per, scan, jnp.int32(1))
    for j in range(UNROLL):
        picked[n + j] = -1
    picked[0] = n - 1

    def finish(j, carry):
        move(0, out_1, started[j], 0).wait()
        return carry

    lax.fori_loop(0, sent, finish, 0)


def apply_kernel(
    source,
    target,
    index,
    picked,
    tiles,
    part_0,
    part_1,
    part_2,
    part_3,
    rights,
    out_stay,
    out_cross,
    out_other_stay,
    out_other_cross,
    held,
    acc,
    blocks,
    copied,
):
    loads = [pltpu.make_async_copy(tiles, held, copied.at[XS])]
    for x, part in enumerate((part_0, part_1, part_2, part_3)):
        at = blocks.at[pl.ds(x * part.shape[0], part.shape[0])]
        loads.append(pltpu.make_async_copy(part, at, copied.at[x]))
    for load in loads:
        load.start()
    half_at, x_at, core_at = (lax.axis_index(a) for a in GRP)
    quarter = out_stay.shape[0]
    count = 4 * quarter

    def read_place(row):
        group = row // ROWS_DEV
        core = (group % CORES) ^ core_at
        x = (x_at - (group // CORES) % XS + XS) % XS
        y = group // (CORES * XS) ^ half_at
        return ((x * CORES + core) * HALVES + y) * ROWS_DEV + row % ROWS_DEV

    def write_place(row):
        group = row // ROWS_DEV
        core = (group % CORES) ^ core_at
        y = group // (CORES * XS) ^ half_at
        x = (group // CORES) % XS
        x = jnp.where(y == 0, (x - x_at + XS) % XS, x)
        return ((core * HALVES + y) * XS + x) * ROWS_DEV + row % ROWS_DEV

    def clear(r, carry):
        acc[r] = jnp.zeros(acc.shape[1:], acc.dtype)
        return carry

    lax.fori_loop(0, count, clear, 0, unroll=4)
    for load in loads:
        load.wait()

    def terms(j, carry):
        for u in range(UNROLL):
            entry = picked[1 + j * UNROLL + u]
            kept = jnp.maximum(entry, 0)
            t = kept // LANES
            slot = kept % LANES
            row = jnp.where(entry < 0, count, write_place(target[t]))
            product = jnp.dot(
                held[slot],
                blocks[read_place(source[t])],
                preferred_element_type=jnp.float32,
            ).astype(jnp.bfloat16)
            acc[row] += jnp.dot(
                product, rights[index[t]], preferred_element_type=jnp.float32
            )
        return carry

    lax.fori_loop(0, (picked[0] + UNROLL - 1) // UNROLL, terms, 0)

    def finish(r, carry):
        for place, out in enumerate(
            (out_stay, out_cross, out_other_stay, out_other_cross)
        ):
            out[r] = acc[place * quarter + r].astype(out.dtype)
        return carry

    lax.fori_loop(0, quarter, finish, 0)


def place_kernel(got, out, copied):
    move = pltpu.make_async_copy(got, out.at[pl.ds(0, got.shape[0])], copied)
    move.start()
    move.wait()


def swap(value, axis):
    return lax.ppermute(value, axis, [(0, 1), (1, 0)])


def add(left, right):
    total = left.astype(jnp.float32) + right.astype(jnp.float32)
    return total.astype(jnp.bfloat16)


def step_x(value, step):
    return lax.ppermute(value, "x", [(i, (i + step) % XS) for i in range(XS)])


def exchange(slots, packing):
    def run(*packed):
        got = lax.all_to_all(packed[slots - 1], ENV, 0, 0, tiled=True)
        if slots == SLOTS:
            return got
        return pl.pallas_call(
            place_kernel,
            out_shape=packing,
            in_specs=[pl.BlockSpec(memory_space=pltpu.VMEM)],
            out_specs=pl.BlockSpec(memory_space=pl.ANY),
            scratch_shapes=[pltpu.SemaphoreType.DMA],
        )(got)

    return run


def shards(
    wavefunction,
    left_tiles,
    right_tiles,
    term_source,
    term_target,
    right_index,
    term_sector,
    column_sector,
):
    per, size, _ = left_tiles.shape
    columns = column_sector.shape[0]
    smem = pl.BlockSpec(memory_space=pltpu.SMEM)
    vmem = pl.BlockSpec(memory_space=pltpu.VMEM)
    anywhere = pl.BlockSpec(memory_space=pl.ANY)
    sectors = term_sector[:, 0]
    slots = columns * SLOTS
    packing = jax.ShapeDtypeStruct((slots, size, size), jnp.bfloat16)

    psi = wavefunction.reshape(-1, size, size)
    across = swap(psi, "y_hi")
    beside = swap(psi, "core")
    *packed, need, picked = pl.pallas_call(
        lambda *refs: pack_kernel(per, *refs),
        out_shape=(
            *[
                jax.ShapeDtypeStruct((columns * (k + 1), size, size), jnp.bfloat16)
                for k in range(SLOTS)
            ],
            jax.ShapeDtypeStruct((1,), jnp.int32),
            jax.ShapeDtypeStruct((sectors.shape[0] + 1 + UNROLL,), jnp.int32),
        ),
        in_specs=[smem, smem, vmem, vmem],
        out_specs=(*[anywhere] * SLOTS, smem, smem),
        scratch_shapes=[pltpu.SMEM((columns,), jnp.int32)] * 3
        + [pltpu.SMEM((slots,), jnp.int32), pltpu.SemaphoreType.DMA((slots,))],
        cost_estimate=pl.CostEstimate(
            flops=0, bytes_accessed=8 * 2**20, transcendentals=0
        ),
    )(sectors, column_sector, sectors.reshape(-1, LANES), left_tiles)
    packed, across = lax.optimization_barrier((packed, across))
    quad = jnp.concatenate([psi, across, beside, swap(across, "core")])
    parts = [quad] + [step_x(quad, step) for step in range(1, XS)]
    tiles = lax.switch(
        need[0] - 1, [exchange(k + 1, packing) for k in range(SLOTS)], *packed
    )
    tiles, parts = lax.optimization_barrier((tiles, parts))
    quarter = quad.shape[0]
    block = jax.ShapeDtypeStruct(quad.shape, jnp.bfloat16)
    stay, cross, other_stay, other_cross = pl.pallas_call(
        apply_kernel,
        out_shape=[block] * 4,
        in_specs=[smem] * 4 + [anywhere] * (1 + XS) + [vmem],
        out_specs=[vmem] * 4,
        scratch_shapes=[
            pltpu.VMEM(packing.shape, jnp.bfloat16),
            pltpu.VMEM((4 * quarter + 1, size, size), jnp.float32),
            pltpu.VMEM((4 * quarter, size, size), jnp.bfloat16),
            pltpu.SemaphoreType.DMA((1 + XS,)),
        ],
        compiler_params=pltpu.CompilerParams(vmem_limit_bytes=40 * 2**20),
    )(
        term_source,
        term_target,
        right_index,
        picked,
        tiles,
        *parts,
        right_tiles,
    )
    cross = add(cross, swap(other_cross, "core"))
    cross = lax.all_to_all(cross, "x", 0, 0, tiled=True)
    cross = jnp.sum(cross.reshape((XS,) + psi.shape).astype(jnp.float32), axis=0)
    crossed = swap(cross.astype(jnp.bfloat16), "y_hi")
    stay = add(stay, swap(other_stay, "core")).reshape((XS,) + psi.shape)
    total = stay[0].astype(jnp.float32)
    for step in range(1, XS):
        total = total + step_x(stay[step], step).astype(jnp.float32)
    total = total + crossed.astype(jnp.float32)
    return total.astype(jnp.bfloat16).reshape(wavefunction.shape)


def solution(mesh):
    physical = Mesh(mesh.devices.reshape(HALVES, XS, CORES, DEEP, LOW), GRP + ENV)
    placed = (
        P(GRP, ENV),
        P(GRP + ENV, None, None),
        P(None, ENV, None),
        P(GRP),
        P(GRP),
        P(GRP),
        P(GRP, None),
        P(),
    )
    return jax.shard_map(
        shards, mesh=physical, in_specs=placed, out_specs=P(GRP, ENV), check_vma=False
    )
```

```python
import jax
import jax.numpy as jnp
from jax import lax
from jax.experimental import pallas as pl
from jax.experimental.pallas import tpu as pltpu
from jax.sharding import Mesh
from jax.sharding import PartitionSpec as P

GRP = ("y_hi", "x", "core")
ENV = ("z", "y_lo")
HALVES, XS, CORES = 2, 4, 2
DEEP, LOW = 8, 4
ROWS_DEV = 4
SLOTS = 4
UNROLL = 16
LANES = 128


def env_place():
    return lax.axis_index("z") * LOW + lax.axis_index("y_lo")


def pack_kernel(
    per,
    sector,
    column,
    sector_rows,
    tiles,
    out_1,
    out_2,
    out_3,
    out_4,
    need,
    picked,
    heads,
    nexts,
    counts,
    started,
    copies,
):
    place = env_place()
    columns = column.shape[0]
    sectors = heads.shape[0]

    rows = sector_rows[...]
    lane = lax.broadcasted_iota(jnp.int32, rows.shape, 1) % per
    rank = jnp.ones(rows.shape, jnp.int32)
    for step in range(1, per):
        same = (pltpu.roll(rows, step, 1) == rows) & (lane >= step)
        rank = rank + same.astype(jnp.int32)
    wanted = rows == column[0]
    for c in range(1, columns):
        wanted = wanted | (rows == column[c])
    slots = jnp.maximum(jnp.max(jnp.where(wanted, rank, 0)), 1)
    need[0] = slots

    def clear(s, carry):
        heads[s] = -1
        counts[s] = 0
        return carry

    lax.fori_loop(0, sectors, clear, 0, unroll=8)

    def chain(c, carry):
        s = column[c]
        nexts[c] = heads[s]
        heads[s] = c
        return carry

    lax.fori_loop(0, columns, chain, 0, unroll=8)

    outs = (out_1, out_2, out_3, out_4)

    def move(i, out, slot, place):
        return pltpu.make_async_copy(tiles.at[i], out.at[place], copies.at[slot])

    def tile(i, n):
        s = sector[place * per + i]
        k = counts[s]
        counts[s] = k + 1

        def send(state):
            c, n = state
            slot = c * slots + k
            for size in range(1, SLOTS + 1):

                @pl.when(slots == size)
                def _(size=size):
                    move(i, outs[size - 1], slot, slot).start()

            started[n] = slot
            return nexts[c], n + 1

        return lax.while_loop(lambda state: state[0] >= 0, send, (heads[s], n))[1]

    sent = lax.fori_loop(0, per, tile, jnp.int32(0))

    mine = column[place]

    def scan(b, n):
        k = b * slots
        for i in range(per):
            t = b * per + i
            match = (sector[t] == mine).astype(jnp.int32)
            picked[n] = t * LANES + k
            n = n + match
            k = k + match
        return n

    n = lax.fori_loop(0, sector.shape[0] // per, scan, jnp.int32(1))
    for j in range(UNROLL):
        picked[n + j] = -1
    picked[0] = n - 1

    def finish(j, carry):
        move(0, out_1, started[j], 0).wait()
        return carry

    lax.fori_loop(0, sent, finish, 0)


def apply_kernel(
    source,
    target,
    index,
    picked,
    need,
    tiles,
    part_0,
    part_1,
    part_2,
    part_3,
    rights,
    out_stay,
    out_cross,
    out_other_stay,
    out_other_cross,
    held,
    acc,
    blocks,
    copied,
):
    size = tiles.shape[0] // SLOTS

    def load_slot(slot):
        at = pl.ds(slot * size, size)
        return pltpu.make_async_copy(tiles.at[at], held.at[at], copied.at[XS + slot])

    for slot in range(SLOTS):

        @pl.when(need[0] > slot)
        def _(slot=slot):
            load_slot(slot).start()

    loads = []
    for x, part in enumerate((part_0, part_1, part_2, part_3)):
        at = blocks.at[pl.ds(x * part.shape[0], part.shape[0])]
        loads.append(pltpu.make_async_copy(part, at, copied.at[x]))
    for load in loads:
        load.start()
    half_at, x_at, core_at = (lax.axis_index(a) for a in GRP)
    quarter = out_stay.shape[0]
    count = 4 * quarter

    def read_place(row):
        group = row // ROWS_DEV
        core = (group % CORES) ^ core_at
        x = (x_at - (group // CORES) % XS + XS) % XS
        y = group // (CORES * XS) ^ half_at
        return ((x * CORES + core) * HALVES + y) * ROWS_DEV + row % ROWS_DEV

    def write_place(row):
        group = row // ROWS_DEV
        core = (group % CORES) ^ core_at
        y = group // (CORES * XS) ^ half_at
        x = (group // CORES) % XS
        x = jnp.where(y == 0, (x - x_at + XS) % XS, x)
        return ((core * HALVES + y) * XS + x) * ROWS_DEV + row % ROWS_DEV

    def clear(r, carry):
        acc[r] = jnp.zeros(acc.shape[1:], acc.dtype)
        return carry

    lax.fori_loop(0, count, clear, 0, unroll=4)
    for load in loads:
        load.wait()
    for slot in range(SLOTS):

        @pl.when(need[0] > slot)
        def _(slot=slot):
            load_slot(slot).wait()

    def terms(j, carry):
        entries = [picked[1 + j * UNROLL + u] for u in range(UNROLL)]
        kept = [jnp.maximum(entry, 0) for entry in entries]
        numbers = [entry // LANES for entry in kept]
        products = [
            jnp.dot(
                held[entry % LANES],
                blocks[read_place(source[t])],
                preferred_element_type=jnp.float32,
            ).astype(jnp.bfloat16)
            for entry, t in zip(kept, numbers)
        ]
        images = [
            jnp.dot(product, rights[index[t]], preferred_element_type=jnp.float32)
            for product, t in zip(products, numbers)
        ]
        for entry, t, image in zip(entries, numbers, images):
            acc[jnp.where(entry < 0, count, write_place(target[t]))] += image
        return carry

    lax.fori_loop(0, (picked[0] + UNROLL - 1) // UNROLL, terms, 0)

    def finish(r, carry):
        for place, out in enumerate(
            (out_stay, out_cross, out_other_stay, out_other_cross)
        ):
            out[r] = acc[place * quarter + r].astype(out.dtype)
        return carry

    lax.fori_loop(0, quarter, finish, 0)


def place_kernel(got, out, copied):
    move = pltpu.make_async_copy(got, out.at[pl.ds(0, got.shape[0])], copied)
    move.start()
    move.wait()


def swap(value, axis):
    return lax.ppermute(value, axis, [(0, 1), (1, 0)])


def add(left, right):
    total = left.astype(jnp.float32) + right.astype(jnp.float32)
    return total.astype(jnp.bfloat16)


def step_x(value, step):
    return lax.ppermute(value, "x", [(i, (i + step) % XS) for i in range(XS)])


def exchange(slots, packing):
    def run(*packed):
        got = lax.all_to_all(packed[slots - 1], ENV, 0, 0, tiled=True)
        if slots == SLOTS:
            return got
        return pl.pallas_call(
            place_kernel,
            out_shape=packing,
            in_specs=[pl.BlockSpec(memory_space=pltpu.VMEM)],
            out_specs=pl.BlockSpec(memory_space=pl.ANY),
            scratch_shapes=[pltpu.SemaphoreType.DMA],
        )(got)

    return run


def shards(
    wavefunction,
    left_tiles,
    right_tiles,
    term_source,
    term_target,
    right_index,
    term_sector,
    column_sector,
):
    per, size, _ = left_tiles.shape
    columns = column_sector.shape[0]
    smem = pl.BlockSpec(memory_space=pltpu.SMEM)
    vmem = pl.BlockSpec(memory_space=pltpu.VMEM)
    anywhere = pl.BlockSpec(memory_space=pl.ANY)
    sectors = term_sector[:, 0]
    slots = columns * SLOTS
    packing = jax.ShapeDtypeStruct((slots, size, size), jnp.bfloat16)

    psi = wavefunction.reshape(-1, size, size)
    across = swap(psi, "y_hi")
    beside = swap(psi, "core")
    *packed, need, picked = pl.pallas_call(
        lambda *refs: pack_kernel(per, *refs),
        out_shape=(
            *[
                jax.ShapeDtypeStruct((columns * (k + 1), size, size), jnp.bfloat16)
                for k in range(SLOTS)
            ],
            jax.ShapeDtypeStruct((1,), jnp.int32),
            jax.ShapeDtypeStruct((sectors.shape[0] + 1 + UNROLL,), jnp.int32),
        ),
        in_specs=[smem, smem, vmem, vmem],
        out_specs=(*[anywhere] * SLOTS, smem, smem),
        scratch_shapes=[pltpu.SMEM((columns,), jnp.int32)] * 3
        + [pltpu.SMEM((slots,), jnp.int32), pltpu.SemaphoreType.DMA((slots,))],
        cost_estimate=pl.CostEstimate(
            flops=0, bytes_accessed=8 * 2**20, transcendentals=0
        ),
    )(sectors, column_sector, sectors.reshape(-1, LANES), left_tiles)
    packed, across = lax.optimization_barrier((packed, across))
    quad = jnp.concatenate([psi, across, beside, swap(across, "core")])
    parts = [quad] + [step_x(quad, step) for step in range(1, XS)]
    tiles = lax.switch(
        need[0] - 1, [exchange(k + 1, packing) for k in range(SLOTS)], *packed
    )
    tiles, parts = lax.optimization_barrier((tiles, parts))
    quarter = quad.shape[0]
    block = jax.ShapeDtypeStruct(quad.shape, jnp.bfloat16)
    stay, cross, other_stay, other_cross = pl.pallas_call(
        apply_kernel,
        out_shape=[block] * 4,
        in_specs=[smem] * 5 + [anywhere] * (1 + XS) + [vmem],
        out_specs=[vmem] * 4,
        scratch_shapes=[
            pltpu.VMEM(packing.shape, jnp.bfloat16),
            pltpu.VMEM((4 * quarter + 1, size, size), jnp.float32),
            pltpu.VMEM((4 * quarter, size, size), jnp.bfloat16),
            pltpu.SemaphoreType.DMA((SLOTS + XS,)),
        ],
        compiler_params=pltpu.CompilerParams(vmem_limit_bytes=40 * 2**20),
    )(
        term_source,
        term_target,
        right_index,
        picked,
        need,
        tiles,
        *parts,
        right_tiles,
    )
    cross = add(cross, swap(other_cross, "core"))
    cross = lax.all_to_all(cross, "x", 0, 0, tiled=True)
    cross = jnp.sum(cross.reshape((XS,) + psi.shape).astype(jnp.float32), axis=0)
    cross = cross.astype(jnp.bfloat16)
    stay = add(stay, swap(other_stay, "core")).reshape((XS,) + psi.shape)
    *early, last = stay
    cross, last = lax.optimization_barrier((cross, last))
    crossed = swap(cross, "y_hi")
    got = [step_x(early[step], step) for step in range(1, XS - 1)]
    got += [step_x(last, XS - 1), crossed]
    total = early[0].astype(jnp.float32)
    for value in got:
        total = total + value.astype(jnp.float32)
    return total.astype(jnp.bfloat16).reshape(wavefunction.shape)


def solution(mesh):
    physical = Mesh(mesh.devices.reshape(HALVES, XS, CORES, DEEP, LOW), GRP + ENV)
    placed = (
        P(GRP, ENV),
        P(GRP + ENV, None, None),
        P(None, ENV, None),
        P(GRP),
        P(GRP),
        P(GRP),
        P(GRP, None),
        P(),
    )
    return jax.shard_map(
        shards, mesh=physical, in_specs=placed, out_specs=P(GRP, ENV), check_vma=False
    )
```

```python
import jax
import jax.numpy as jnp
from jax import lax
from jax.experimental import pallas as pl
from jax.experimental.pallas import tpu as pltpu
from jax.sharding import Mesh
from jax.sharding import PartitionSpec as P

GRP = ("y_hi", "x", "core")
ENV = ("z", "y_lo")
HALVES, XS, CORES = 2, 4, 2
DEEP, LOW = 8, 4
ROWS_DEV = 4
SLOTS = 4
UNROLL = 16
LANES = 128


def env_place():
    return lax.axis_index("z") * LOW + lax.axis_index("y_lo")


def pack_kernel(
    per,
    sector,
    column,
    sector_rows,
    tiles,
    out_1,
    out_2,
    out_3,
    out_4,
    need,
    picked,
    heads,
    nexts,
    counts,
    started,
    copies,
):
    place = env_place()
    columns = column.shape[0]
    sectors = heads.shape[0]

    rows = sector_rows[...]
    lane = lax.broadcasted_iota(jnp.int32, rows.shape, 1) % per
    rank = jnp.ones(rows.shape, jnp.int32)
    for step in range(1, per):
        same = (pltpu.roll(rows, step, 1) == rows) & (lane >= step)
        rank = rank + same.astype(jnp.int32)
    wanted = rows == column[0]
    for c in range(1, columns):
        wanted = wanted | (rows == column[c])
    slots = jnp.maximum(jnp.max(jnp.where(wanted, rank, 0)), 1)
    need[0] = slots

    def clear(s, carry):
        heads[s] = -1
        counts[s] = 0
        return carry

    lax.fori_loop(0, sectors, clear, 0, unroll=8)

    def chain(c, carry):
        s = column[c]
        nexts[c] = heads[s]
        heads[s] = c
        return carry

    lax.fori_loop(0, columns, chain, 0, unroll=8)

    outs = (out_1, out_2, out_3, out_4)

    def move(i, out, slot, place):
        return pltpu.make_async_copy(tiles.at[i], out.at[place], copies.at[slot])

    def tile(i, n):
        s = sector[place * per + i]
        k = counts[s]
        counts[s] = k + 1

        def send(state):
            c, n = state
            slot = c * slots + k
            for size in range(1, SLOTS + 1):

                @pl.when(slots == size)
                def _(size=size):
                    move(i, outs[size - 1], slot, slot).start()

            started[n] = slot
            return nexts[c], n + 1

        return lax.while_loop(lambda state: state[0] >= 0, send, (heads[s], n))[1]

    sent = lax.fori_loop(0, per, tile, jnp.int32(0))

    mine = column[place]

    def scan(b, n):
        k = b * slots
        for i in range(per):
            t = b * per + i
            match = (sector[t] == mine).astype(jnp.int32)
            picked[n] = t * LANES + k
            n = n + match
            k = k + match
        return n

    n = lax.fori_loop(0, sector.shape[0] // per, scan, jnp.int32(1))
    for j in range(UNROLL):
        picked[n + j] = -1
    picked[0] = n - 1

    def finish(j, carry):
        move(0, out_1, started[j], 0).wait()
        return carry

    lax.fori_loop(0, sent, finish, 0)


def apply_kernel(
    source,
    target,
    index,
    picked,
    need,
    tiles,
    part_0,
    part_1,
    part_2,
    part_3,
    rights,
    out_stay,
    out_cross,
    out_other_stay,
    out_other_cross,
    held,
    acc,
    blocks,
    copied,
):
    size = tiles.shape[0] // SLOTS

    def load_slot(slot):
        at = pl.ds(slot * size, size)
        return pltpu.make_async_copy(tiles.at[at], held.at[at], copied.at[XS + slot])

    for slot in range(SLOTS):

        @pl.when(need[0] > slot)
        def _(slot=slot):
            load_slot(slot).start()

    loads = []
    for x, part in enumerate((part_0, part_1, part_2, part_3)):
        at = blocks.at[pl.ds(x * part.shape[0], part.shape[0])]
        loads.append(pltpu.make_async_copy(part, at, copied.at[x]))
    for load in loads:
        load.start()
    half_at, x_at, core_at = (lax.axis_index(a) for a in GRP)
    quarter = out_stay.shape[0]
    count = 4 * quarter

    def read_place(row):
        group = row // ROWS_DEV
        core = (group % CORES) ^ core_at
        x = (x_at - (group // CORES) % XS + XS) % XS
        y = group // (CORES * XS) ^ half_at
        return ((x * CORES + core) * HALVES + y) * ROWS_DEV + row % ROWS_DEV

    def write_place(row):
        group = row // ROWS_DEV
        core = (group % CORES) ^ core_at
        y = group // (CORES * XS) ^ half_at
        x = (group // CORES) % XS
        x = jnp.where(y == 0, (x - x_at + XS) % XS, x)
        return ((core * HALVES + y) * XS + x) * ROWS_DEV + row % ROWS_DEV

    def clear(r, carry):
        acc[r] = jnp.zeros(acc.shape[1:], acc.dtype)
        return carry

    lax.fori_loop(0, count, clear, 0, unroll=4)
    for load in loads:
        load.wait()
    def arrive(slot, carry):
        load_slot(slot).wait()
        return carry

    def terms(j, here):
        last = picked[jnp.minimum((j + 1) * UNROLL, picked[0])]
        wanted = (last % LANES) // size + 1
        lax.fori_loop(here, wanted, arrive, 0)
        entries = [picked[1 + j * UNROLL + u] for u in range(UNROLL)]
        kept = [jnp.maximum(entry, 0) for entry in entries]
        numbers = [entry // LANES for entry in kept]
        products = [
            jnp.dot(
                held[entry % LANES],
                blocks[read_place(source[t])],
                preferred_element_type=jnp.float32,
            ).astype(jnp.bfloat16)
            for entry, t in zip(kept, numbers)
        ]
        images = [
            jnp.dot(product, rights[index[t]], preferred_element_type=jnp.float32)
            for product, t in zip(products, numbers)
        ]
        for entry, t, image in zip(entries, numbers, images):
            acc[jnp.where(entry < 0, count, write_place(target[t]))] += image
        return jnp.maximum(here, wanted)

    here = lax.fori_loop(
        0, (picked[0] + UNROLL - 1) // UNROLL, terms, jnp.int32(0)
    )
    lax.fori_loop(here, need[0], arrive, 0)

    def finish(r, carry):
        for place, out in enumerate(
            (out_stay, out_cross, out_other_stay, out_other_cross)
        ):
            out[r] = acc[place * quarter + r].astype(out.dtype)
        return carry

    lax.fori_loop(0, quarter, finish, 0)


def place_kernel(got, out, copied):
    move = pltpu.make_async_copy(got, out.at[pl.ds(0, got.shape[0])], copied)
    move.start()
    move.wait()


def swap(value, axis):
    return lax.ppermute(value, axis, [(0, 1), (1, 0)])


def add(left, right):
    total = left.astype(jnp.float32) + right.astype(jnp.float32)
    return total.astype(jnp.bfloat16)


def step_x(value, step):
    return lax.ppermute(value, "x", [(i, (i + step) % XS) for i in range(XS)])


def exchange(slots, packing):
    def run(*packed):
        got = lax.all_to_all(packed[slots - 1], ENV, 0, 0, tiled=True)
        if slots == SLOTS:
            return got
        return pl.pallas_call(
            place_kernel,
            out_shape=packing,
            in_specs=[pl.BlockSpec(memory_space=pltpu.VMEM)],
            out_specs=pl.BlockSpec(memory_space=pl.ANY),
            scratch_shapes=[pltpu.SemaphoreType.DMA],
        )(got)

    return run


def shards(
    wavefunction,
    left_tiles,
    right_tiles,
    term_source,
    term_target,
    right_index,
    term_sector,
    column_sector,
):
    per, size, _ = left_tiles.shape
    columns = column_sector.shape[0]
    smem = pl.BlockSpec(memory_space=pltpu.SMEM)
    vmem = pl.BlockSpec(memory_space=pltpu.VMEM)
    anywhere = pl.BlockSpec(memory_space=pl.ANY)
    sectors = term_sector[:, 0]
    slots = columns * SLOTS
    packing = jax.ShapeDtypeStruct((slots, size, size), jnp.bfloat16)

    psi = wavefunction.reshape(-1, size, size)
    across = swap(psi, "y_hi")
    beside = swap(psi, "core")
    *packed, need, picked = pl.pallas_call(
        lambda *refs: pack_kernel(per, *refs),
        out_shape=(
            *[
                jax.ShapeDtypeStruct((columns * (k + 1), size, size), jnp.bfloat16)
                for k in range(SLOTS)
            ],
            jax.ShapeDtypeStruct((1,), jnp.int32),
            jax.ShapeDtypeStruct((sectors.shape[0] + 1 + UNROLL,), jnp.int32),
        ),
        in_specs=[smem, smem, vmem, vmem],
        out_specs=(*[anywhere] * SLOTS, smem, smem),
        scratch_shapes=[pltpu.SMEM((columns,), jnp.int32)] * 3
        + [pltpu.SMEM((slots,), jnp.int32), pltpu.SemaphoreType.DMA((slots,))],
        cost_estimate=pl.CostEstimate(
            flops=0, bytes_accessed=8 * 2**20, transcendentals=0
        ),
    )(sectors, column_sector, sectors.reshape(-1, LANES), left_tiles)
    packed, across = lax.optimization_barrier((packed, across))
    quad = jnp.concatenate([psi, across, beside, swap(across, "core")])
    parts = [quad] + [step_x(quad, step) for step in range(1, XS)]
    tiles = lax.switch(
        need[0] - 1, [exchange(k + 1, packing) for k in range(SLOTS)], *packed
    )
    tiles, parts = lax.optimization_barrier((tiles, parts))
    quarter = quad.shape[0]
    block = jax.ShapeDtypeStruct(quad.shape, jnp.bfloat16)
    stay, cross, other_stay, other_cross = pl.pallas_call(
        apply_kernel,
        out_shape=[block] * 4,
        in_specs=[smem] * 5 + [anywhere] * (1 + XS) + [vmem],
        out_specs=[vmem] * 4,
        scratch_shapes=[
            pltpu.VMEM(packing.shape, jnp.bfloat16),
            pltpu.VMEM((4 * quarter + 1, size, size), jnp.float32),
            pltpu.VMEM((4 * quarter, size, size), jnp.bfloat16),
            pltpu.SemaphoreType.DMA((SLOTS + XS,)),
        ],
        compiler_params=pltpu.CompilerParams(vmem_limit_bytes=40 * 2**20),
    )(
        term_source,
        term_target,
        right_index,
        picked,
        need,
        tiles,
        *parts,
        right_tiles,
    )
    cross = add(cross, swap(other_cross, "core"))
    cross = lax.all_to_all(cross, "x", 0, 0, tiled=True)
    cross = jnp.sum(cross.reshape((XS,) + psi.shape).astype(jnp.float32), axis=0)
    cross = cross.astype(jnp.bfloat16)
    stay = add(stay, swap(other_stay, "core")).reshape((XS,) + psi.shape)
    *early, last = stay
    cross, last = lax.optimization_barrier((cross, last))
    crossed = swap(cross, "y_hi")
    got = [step_x(early[step], step) for step in range(1, XS - 1)]
    got += [step_x(last, XS - 1), crossed]
    total = early[0].astype(jnp.float32)
    for value in got:
        total = total + value.astype(jnp.float32)
    return total.astype(jnp.bfloat16).reshape(wavefunction.shape)


def solution(mesh):
    physical = Mesh(mesh.devices.reshape(HALVES, XS, CORES, DEEP, LOW), GRP + ENV)
    placed = (
        P(GRP, ENV),
        P(GRP + ENV, None, None),
        P(None, ENV, None),
        P(GRP),
        P(GRP),
        P(GRP),
        P(GRP, None),
        P(),
    )
    return jax.shard_map(
        shards, mesh=physical, in_specs=placed, out_specs=P(GRP, ENV), check_vma=False
    )
```

```python
import jax
import jax.numpy as jnp
from jax import lax
from jax.experimental import pallas as pl
from jax.experimental.pallas import tpu as pltpu
from jax.sharding import Mesh
from jax.sharding import PartitionSpec as P

GRP = ("y_hi", "x", "core")
ENV = ("z", "y_lo")
HALVES, XS, CORES = 2, 4, 2
DEEP, LOW = 8, 4
ROWS_DEV = 4
SLOTS = 4
UNROLL = 16
LANES = 128


def env_place():
    return lax.axis_index("z") * LOW + lax.axis_index("y_lo")


def split(row):
    return row >> 5, row >> 3 & 3, row >> 2 & 1, row & 3


def read_place(row):
    half_at, x_at, _ = (lax.axis_index(a) for a in GRP)
    y, x, core, rest = split(row)
    return (x_at - x & 3) << 4 | core << 3 | (y ^ half_at) << 2 | rest


def write_place(row):
    half_at, x_at, core_at = (lax.axis_index(a) for a in GRP)
    y, x, core, rest = split(row)
    y = y ^ half_at
    x = jnp.where(y == 0, x - x_at & 3, x)
    return (core ^ core_at) << 5 | y << 4 | x << 2 | rest


def word_of(slot, index, row, block):
    return slot | index << 7 | row << 12 | block << 19


def parts_of(word):
    return word & 127, word >> 7 & 31, word >> 12 & 127, word >> 19


def pack_kernel(
    per,
    sector,
    column,
    source,
    target,
    index,
    sector_rows,
    tiles,
    out_1,
    out_2,
    out_3,
    out_4,
    need,
    picked,
    heads,
    nexts,
    counts,
    started,
    copies,
):
    place = env_place()
    columns = column.shape[0]
    sectors = heads.shape[0]

    rows = sector_rows[...]
    lane = lax.broadcasted_iota(jnp.int32, rows.shape, 1) % per
    rank = jnp.ones(rows.shape, jnp.int32)
    for step in range(1, per):
        same = (pltpu.roll(rows, step, 1) == rows) & (lane >= step)
        rank = rank + same.astype(jnp.int32)
    wanted = rows == column[0]
    for c in range(1, columns):
        wanted = wanted | (rows == column[c])
    slots = jnp.maximum(jnp.max(jnp.where(wanted, rank, 0)), 1)
    need[0] = slots

    def clear(s, carry):
        heads[s] = -1
        counts[s] = 0
        return carry

    lax.fori_loop(0, sectors, clear, 0, unroll=8)

    def chain(c, carry):
        s = column[c]
        nexts[c] = heads[s]
        heads[s] = c
        return carry

    lax.fori_loop(0, columns, chain, 0, unroll=8)

    outs = (out_1, out_2, out_3, out_4)

    def move(i, out, slot, place):
        return pltpu.make_async_copy(tiles.at[i], out.at[place], copies.at[slot])

    def tile(i, n):
        s = sector[place * per + i]
        k = counts[s]
        counts[s] = k + 1

        def send(state):
            c, n = state
            slot = c * slots + k
            for size in range(1, SLOTS + 1):

                @pl.when(slots == size)
                def _(size=size):
                    move(i, outs[size - 1], slot, slot).start()

            started[n] = slot
            return nexts[c], n + 1

        return lax.while_loop(lambda state: state[0] >= 0, send, (heads[s], n))[1]

    sent = lax.fori_loop(0, per, tile, jnp.int32(0))

    mine = column[place]

    def scan(b, n):
        k = b * slots
        for i in range(per):
            t = b * per + i
            match = (sector[t] == mine).astype(jnp.int32)
            picked[n] = t * LANES + k
            n = n + match
            k = k + match
        return n

    n = lax.fori_loop(0, sector.shape[0] // per, scan, jnp.int32(1))
    spare = HALVES * XS * CORES * ROWS_DEV
    for j in range(UNROLL):
        picked[n + j] = word_of(0, 0, spare, 0)
    picked[0] = n - 1

    def resolve(j, carry):
        t = picked[j] >> 7
        row, block = write_place(target[t]), read_place(source[t])
        picked[j] = word_of(picked[j] & 127, index[t], row, block)
        return carry

    lax.fori_loop(1, n, resolve, 0)

    def finish(j, carry):
        move(0, out_1, started[j], 0).wait()
        return carry

    lax.fori_loop(0, sent, finish, 0)


def apply_kernel(
    picked,
    need,
    tiles,
    part_0,
    part_1,
    part_2,
    part_3,
    rights,
    out_stay,
    out_cross,
    out_other_stay,
    out_other_cross,
    held,
    acc,
    blocks,
    copied,
):
    size = tiles.shape[0] // SLOTS

    def load_slot(slot):
        at = pl.ds(slot * size, size)
        return pltpu.make_async_copy(tiles.at[at], held.at[at], copied.at[XS + slot])

    for slot in range(SLOTS):

        @pl.when(need[0] > slot)
        def _(slot=slot):
            load_slot(slot).start()

    loads = []
    for x, part in enumerate((part_0, part_1, part_2, part_3)):
        at = blocks.at[pl.ds(x * part.shape[0], part.shape[0])]
        loads.append(pltpu.make_async_copy(part, at, copied.at[x]))
    for load in loads:
        load.start()
    quarter = out_stay.shape[0]
    count = 4 * quarter

    def clear(r, carry):
        acc[r] = jnp.zeros(acc.shape[1:], acc.dtype)
        return carry

    lax.fori_loop(0, count, clear, 0, unroll=4)
    for load in loads:
        load.wait()

    def arrive(slot, carry):
        load_slot(slot).wait()
        return carry

    def terms(j, here):
        last = picked[jnp.minimum((j + 1) * UNROLL, picked[0])]
        wanted = lax.div(parts_of(last)[0], jnp.int32(size)) + 1
        lax.fori_loop(here, wanted, arrive, 0)
        words = [parts_of(picked[1 + j * UNROLL + u]) for u in range(UNROLL)]
        products = [
            jnp.dot(
                held[slot], blocks[block], preferred_element_type=jnp.float32
            ).astype(jnp.bfloat16)
            for slot, _, _, block in words
        ]
        images = [
            jnp.dot(product, rights[tile], preferred_element_type=jnp.float32)
            for product, (_, tile, _, _) in zip(products, words)
        ]
        for (_, _, row, _), image in zip(words, images):
            acc[row] += image
        return jnp.maximum(here, wanted)

    here = lax.fori_loop(
        0, (picked[0] + UNROLL - 1) // UNROLL, terms, jnp.int32(0)
    )
    lax.fori_loop(here, need[0], arrive, 0)

    def finish(r, carry):
        for place, out in enumerate(
            (out_stay, out_cross, out_other_stay, out_other_cross)
        ):
            out[r] = acc[place * quarter + r].astype(out.dtype)
        return carry

    lax.fori_loop(0, quarter, finish, 0)


def place_kernel(got, out, copied):
    move = pltpu.make_async_copy(got, out.at[pl.ds(0, got.shape[0])], copied)
    move.start()
    move.wait()


def swap(value, axis):
    return lax.ppermute(value, axis, [(0, 1), (1, 0)])


def add(left, right):
    total = left.astype(jnp.float32) + right.astype(jnp.float32)
    return total.astype(jnp.bfloat16)


def step_x(value, step):
    return lax.ppermute(value, "x", [(i, (i + step) % XS) for i in range(XS)])


def exchange(slots, packing):
    def run(*packed):
        got = lax.all_to_all(packed[slots - 1], ENV, 0, 0, tiled=True)
        if slots == SLOTS:
            return got
        return pl.pallas_call(
            place_kernel,
            out_shape=packing,
            in_specs=[pl.BlockSpec(memory_space=pltpu.VMEM)],
            out_specs=pl.BlockSpec(memory_space=pl.ANY),
            scratch_shapes=[pltpu.SemaphoreType.DMA],
        )(got)

    return run


def shards(
    wavefunction,
    left_tiles,
    right_tiles,
    term_source,
    term_target,
    right_index,
    term_sector,
    column_sector,
):
    per, size, _ = left_tiles.shape
    columns = column_sector.shape[0]
    smem = pl.BlockSpec(memory_space=pltpu.SMEM)
    vmem = pl.BlockSpec(memory_space=pltpu.VMEM)
    anywhere = pl.BlockSpec(memory_space=pl.ANY)
    sectors = term_sector[:, 0]
    slots = columns * SLOTS
    packing = jax.ShapeDtypeStruct((slots, size, size), jnp.bfloat16)

    psi = wavefunction.reshape(-1, size, size)
    across = swap(psi, "y_hi")
    *packed, need, picked = pl.pallas_call(
        lambda *refs: pack_kernel(per, *refs),
        out_shape=(
            *[
                jax.ShapeDtypeStruct((columns * (k + 1), size, size), jnp.bfloat16)
                for k in range(SLOTS)
            ],
            jax.ShapeDtypeStruct((1,), jnp.int32),
            jax.ShapeDtypeStruct((sectors.shape[0] + 1 + UNROLL,), jnp.int32),
        ),
        in_specs=[smem] * 5 + [vmem] * 2,
        out_specs=(*[anywhere] * SLOTS, smem, smem),
        scratch_shapes=[pltpu.SMEM((columns,), jnp.int32)] * 3
        + [pltpu.SMEM((slots,), jnp.int32), pltpu.SemaphoreType.DMA((slots,))],
        cost_estimate=pl.CostEstimate(
            flops=0, bytes_accessed=8 * 2**20, transcendentals=0
        ),
    )(
        sectors,
        column_sector,
        term_source,
        term_target,
        right_index,
        sectors.reshape(-1, LANES),
        left_tiles,
    )
    packed, across = lax.optimization_barrier((packed, across))
    pair = jnp.concatenate([psi, across])
    quad = lax.all_gather(pair, "core", axis=0, tiled=True)
    parts = [quad] + [step_x(quad, step) for step in range(1, XS)]
    tiles = lax.switch(
        need[0] - 1, [exchange(k + 1, packing) for k in range(SLOTS)], *packed
    )
    tiles, parts = lax.optimization_barrier((tiles, parts))
    quarter = quad.shape[0]
    block = jax.ShapeDtypeStruct(quad.shape, jnp.bfloat16)
    stay, cross, other_stay, other_cross = pl.pallas_call(
        apply_kernel,
        out_shape=[block] * 4,
        in_specs=[smem] * 2 + [anywhere] * (1 + XS) + [vmem],
        out_specs=[vmem] * 4,
        scratch_shapes=[
            pltpu.VMEM(packing.shape, jnp.bfloat16),
            pltpu.VMEM((4 * quarter + 1, size, size), jnp.float32),
            pltpu.VMEM((4 * quarter, size, size), jnp.bfloat16),
            pltpu.SemaphoreType.DMA((SLOTS + XS,)),
        ],
        compiler_params=pltpu.CompilerParams(vmem_limit_bytes=40 * 2**20),
    )(
        picked,
        need,
        tiles,
        *parts,
        right_tiles,
    )
    cross = add(cross, swap(other_cross, "core"))
    cross = lax.all_to_all(cross, "x", 0, 0, tiled=True)
    cross = jnp.sum(cross.reshape((XS,) + psi.shape).astype(jnp.float32), axis=0)
    cross = cross.astype(jnp.bfloat16)
    stay = add(stay, swap(other_stay, "core")).reshape((XS,) + psi.shape)
    *early, last = stay
    cross, last = lax.optimization_barrier((cross, last))
    crossed = swap(cross, "y_hi")
    got = [step_x(early[step], step) for step in range(1, XS - 1)]
    got += [step_x(last, XS - 1), crossed]
    total = early[0].astype(jnp.float32)
    for value in got:
        total = total + value.astype(jnp.float32)
    return total.astype(jnp.bfloat16).reshape(wavefunction.shape)


def solution(mesh):
    physical = Mesh(mesh.devices.reshape(HALVES, XS, CORES, DEEP, LOW), GRP + ENV)
    placed = (
        P(GRP, ENV),
        P(GRP + ENV, None, None),
        P(None, ENV, None),
        P(GRP),
        P(GRP),
        P(GRP),
        P(GRP, None),
        P(),
    )
    return jax.shard_map(
        shards, mesh=physical, in_specs=placed, out_specs=P(GRP, ENV), check_vma=False
    )
```

```python
import jax
import jax.numpy as jnp
from jax import lax
from jax.experimental import pallas as pl
from jax.experimental.pallas import tpu as pltpu
from jax.sharding import Mesh
from jax.sharding import PartitionSpec as P

GRP = ("y_hi", "x", "core")
ENV = ("z", "y_lo")
HALVES, XS, CORES = 2, 4, 2
DEEP, LOW = 8, 4
ROWS_DEV = 4
SLOTS = 4
UNROLL = 16
LANES = 128


def env_place():
    return lax.axis_index("z") * LOW + lax.axis_index("y_lo")


def split(row):
    return row >> 5, row >> 3 & 3, row >> 2 & 1, row & 3


def read_place(row):
    half_at, x_at, _ = (lax.axis_index(a) for a in GRP)
    y, x, core, rest = split(row)
    return (x_at - x & 3) << 4 | core << 3 | (y ^ half_at) << 2 | rest


def write_place(row):
    half_at, x_at, core_at = (lax.axis_index(a) for a in GRP)
    y, x, core, rest = split(row)
    y = y ^ half_at
    x = jnp.where(y == 0, x - x_at & 3, x)
    return (core ^ core_at) << 5 | y << 4 | x << 2 | rest


def word_of(slot, index, row, block):
    return slot | index << 7 | row << 12 | block << 19


def parts_of(word):
    return word & 127, word >> 7 & 31, word >> 12 & 127, word >> 19


def pack_kernel(
    per,
    sector,
    column,
    source,
    target,
    index,
    sector_rows,
    tiles,
    out_1,
    out_2,
    out_3,
    out_4,
    need,
    picked,
    heads,
    nexts,
    counts,
    started,
    copies,
):
    place = env_place()
    columns = column.shape[0]
    sectors = heads.shape[0]

    rows = sector_rows[...]
    lane = lax.broadcasted_iota(jnp.int32, rows.shape, 1) % per
    rank = jnp.ones(rows.shape, jnp.int32)
    for step in range(1, per):
        same = (pltpu.roll(rows, step, 1) == rows) & (lane >= step)
        rank = rank + same.astype(jnp.int32)
    wanted = rows == column[0]
    for c in range(1, columns):
        wanted = wanted | (rows == column[c])
    slots = jnp.maximum(jnp.max(jnp.where(wanted, rank, 0)), 1)
    need[0] = slots

    def clear(s, carry):
        heads[s] = -1
        counts[s] = 0
        return carry

    lax.fori_loop(0, sectors, clear, 0, unroll=8)

    def chain(c, carry):
        s = column[c]
        nexts[c] = heads[s]
        heads[s] = c
        return carry

    lax.fori_loop(0, columns, chain, 0, unroll=8)

    outs = (out_1, out_2, out_3, out_4)

    def move(i, out, slot, place):
        return pltpu.make_async_copy(tiles.at[i], out.at[place], copies.at[slot])

    def tile(i, n):
        s = sector[place * per + i]
        k = counts[s]
        counts[s] = k + 1

        def send(state):
            c, n = state
            slot = c * slots + k
            for size in range(1, SLOTS + 1):

                @pl.when(slots == size)
                def _(size=size):
                    move(i, outs[size - 1], slot, slot).start()

            started[n] = slot
            return nexts[c], n + 1

        return lax.while_loop(lambda state: state[0] >= 0, send, (heads[s], n))[1]

    sent = lax.fori_loop(0, per, tile, jnp.int32(0))

    mine = column[place]

    def scan(b, n):
        k = b * slots
        for i in range(per):
            t = b * per + i
            match = (sector[t] == mine).astype(jnp.int32)
            picked[n] = t * LANES + k
            n = n + match
            k = k + match
        return n

    n = lax.fori_loop(0, sector.shape[0] // per, scan, jnp.int32(1))
    spare = HALVES * XS * CORES * ROWS_DEV
    for j in range(UNROLL):
        picked[n + j] = word_of(0, 0, spare, 0)
    picked[0] = n - 1

    def resolve(j, carry):
        t = picked[j] >> 7
        row, block = write_place(target[t]), read_place(source[t])
        picked[j] = word_of(picked[j] & 127, index[t], row, block)
        return carry

    lax.fori_loop(1, n, resolve, 0)

    def finish(j, carry):
        move(0, out_1, started[j], 0).wait()
        return carry

    lax.fori_loop(0, sent, finish, 0)


def apply_kernel(
    picked,
    need,
    tiles,
    part_0,
    part_1,
    part_2,
    part_3,
    rights,
    out_stay,
    out_cross,
    out_other_stay,
    out_other_cross,
    held,
    acc,
    blocks,
    copied,
):
    size = tiles.shape[0] // SLOTS

    def load_slot(slot):
        at = pl.ds(slot * size, size)
        return pltpu.make_async_copy(tiles.at[at], held.at[at], copied.at[XS + slot])

    for slot in range(SLOTS):

        @pl.when(need[0] > slot)
        def _(slot=slot):
            load_slot(slot).start()

    loads = []
    for x, part in enumerate((part_0, part_1, part_2, part_3)):
        at = blocks.at[pl.ds(x * part.shape[0], part.shape[0])]
        loads.append(pltpu.make_async_copy(part, at, copied.at[x]))
    for load in loads:
        load.start()
    quarter = out_stay.shape[0]
    count = 4 * quarter

    def clear(r, carry):
        acc[r] = jnp.zeros(acc.shape[1:], acc.dtype)
        return carry

    lax.fori_loop(0, count, clear, 0, unroll=4)
    for load in loads:
        load.wait()

    def arrive(slot, carry):
        load_slot(slot).wait()
        return carry

    def terms(j, here):
        last = picked[jnp.minimum((j + 1) * UNROLL, picked[0])]
        wanted = lax.div(parts_of(last)[0], jnp.int32(size)) + 1
        lax.fori_loop(here, wanted, arrive, 0)
        words = [parts_of(picked[1 + j * UNROLL + u]) for u in range(UNROLL)]
        products = [
            jnp.dot(
                held[slot], blocks[block], preferred_element_type=jnp.float32
            ).astype(jnp.bfloat16)
            for slot, _, _, block in words
        ]
        images = [
            jnp.dot(product, rights[tile], preferred_element_type=jnp.float32)
            for product, (_, tile, _, _) in zip(products, words)
        ]
        for (_, _, row, _), image in zip(words, images):
            acc[row] += image
        return jnp.maximum(here, wanted)

    here = lax.fori_loop(
        0, (picked[0] + UNROLL - 1) // UNROLL, terms, jnp.int32(0)
    )
    lax.fori_loop(here, need[0], arrive, 0)

    def finish(r, carry):
        for place, out in enumerate(
            (out_stay, out_cross, out_other_stay, out_other_cross)
        ):
            out[r] = acc[place * quarter + r].astype(out.dtype)
        return carry

    lax.fori_loop(0, quarter, finish, 0)


def place_kernel(got, out, copied):
    move = pltpu.make_async_copy(got, out.at[pl.ds(0, got.shape[0])], copied)
    move.start()
    move.wait()


def swap(value, axis):
    return lax.ppermute(value, axis, [(0, 1), (1, 0)])


def add(left, right):
    total = left.astype(jnp.float32) + right.astype(jnp.float32)
    return total.astype(jnp.bfloat16)


def step_x(value, step):
    return lax.ppermute(value, "x", [(i, (i + step) % XS) for i in range(XS)])


def exchange(slots, packing):
    def run(*packed):
        got = lax.all_to_all(packed[slots - 1], ENV, 0, 0, tiled=True)
        if slots == SLOTS:
            return got
        return pl.pallas_call(
            place_kernel,
            out_shape=packing,
            in_specs=[pl.BlockSpec(memory_space=pltpu.VMEM)],
            out_specs=pl.BlockSpec(memory_space=pl.ANY),
            scratch_shapes=[pltpu.SemaphoreType.DMA],
        )(got)

    return run


def shards(
    wavefunction,
    left_tiles,
    right_tiles,
    term_source,
    term_target,
    right_index,
    term_sector,
    column_sector,
):
    per, size, _ = left_tiles.shape
    columns = column_sector.shape[0]
    smem = pl.BlockSpec(memory_space=pltpu.SMEM)
    vmem = pl.BlockSpec(memory_space=pltpu.VMEM)
    anywhere = pl.BlockSpec(memory_space=pl.ANY)
    sectors = term_sector[:, 0]
    slots = columns * SLOTS
    packing = jax.ShapeDtypeStruct((slots, size, size), jnp.bfloat16)

    psi = wavefunction.reshape(-1, size, size)
    across = swap(psi, "y_hi")
    *packed, need, picked = pl.pallas_call(
        lambda *refs: pack_kernel(per, *refs),
        out_shape=(
            *[
                jax.ShapeDtypeStruct((columns * (k + 1), size, size), jnp.bfloat16)
                for k in range(SLOTS)
            ],
            jax.ShapeDtypeStruct((1,), jnp.int32),
            jax.ShapeDtypeStruct((sectors.shape[0] + 1 + UNROLL,), jnp.int32),
        ),
        in_specs=[smem] * 5 + [vmem] * 2,
        out_specs=(*[anywhere] * SLOTS, smem, smem),
        scratch_shapes=[pltpu.SMEM((columns,), jnp.int32)] * 3
        + [pltpu.SMEM((slots,), jnp.int32), pltpu.SemaphoreType.DMA((slots,))],
        cost_estimate=pl.CostEstimate(
            flops=0, bytes_accessed=8 * 2**20, transcendentals=0
        ),
    )(
        sectors,
        column_sector,
        term_source,
        term_target,
        right_index,
        sectors.reshape(-1, LANES),
        left_tiles,
    )
    packed, across = lax.optimization_barrier((packed, across))
    pair = jnp.concatenate([psi, across])
    quad = lax.all_gather(pair, "core", axis=0, tiled=True)
    parts = [quad] + [step_x(quad, step) for step in range(1, XS)]
    tiles = lax.switch(
        need[0] - 1, [exchange(k + 1, packing) for k in range(SLOTS)], *packed
    )
    tiles, parts = lax.optimization_barrier((tiles, parts))
    quarter = quad.shape[0]
    block = jax.ShapeDtypeStruct(quad.shape, jnp.bfloat16)
    stay, cross, other_stay, other_cross = pl.pallas_call(
        apply_kernel,
        out_shape=[block] * 4,
        in_specs=[smem] * 2 + [anywhere] * (1 + XS) + [vmem],
        out_specs=[vmem] * 4,
        scratch_shapes=[
            pltpu.VMEM(packing.shape, jnp.bfloat16),
            pltpu.VMEM((4 * quarter + 1, size, size), jnp.float32),
            pltpu.VMEM((4 * quarter, size, size), jnp.bfloat16),
            pltpu.SemaphoreType.DMA((SLOTS + XS,)),
        ],
        compiler_params=pltpu.CompilerParams(vmem_limit_bytes=40 * 2**20),
    )(
        picked,
        need,
        tiles,
        *parts,
        right_tiles,
    )
    cross = add(cross, swap(other_cross, "core"))
    cross = lax.all_to_all(cross, "x", 0, 0, tiled=True)
    cross = jnp.sum(cross.reshape((XS,) + psi.shape).astype(jnp.float32), axis=0)
    cross = cross.astype(jnp.bfloat16)
    stay = add(stay, swap(other_stay, "core")).reshape((XS,) + psi.shape)
    *early, last = stay
    crossed = swap(cross, "y_hi")
    total = early[0].astype(jnp.float32)
    for step in range(1, XS - 1):
        total = total + step_x(early[step], step).astype(jnp.float32)
    cross, total, last = lax.optimization_barrier((cross, total, last))
    total = total + step_x(last, XS - 1).astype(jnp.float32)
    total = total + crossed.astype(jnp.float32)
    return total.astype(jnp.bfloat16).reshape(wavefunction.shape)


def solution(mesh):
    physical = Mesh(mesh.devices.reshape(HALVES, XS, CORES, DEEP, LOW), GRP + ENV)
    placed = (
        P(GRP, ENV),
        P(GRP + ENV, None, None),
        P(None, ENV, None),
        P(GRP),
        P(GRP),
        P(GRP),
        P(GRP, None),
        P(),
    )
    return jax.shard_map(
        shards, mesh=physical, in_specs=placed, out_specs=P(GRP, ENV), check_vma=False
    )
```

```python
import jax
import jax.numpy as jnp
from jax import lax
from jax.experimental import pallas as pl
from jax.experimental.pallas import tpu as pltpu
from jax.sharding import Mesh
from jax.sharding import PartitionSpec as P

GRP = ("y_hi", "x", "core")
ENV = ("z", "y_lo")
HALVES, XS, CORES = 2, 4, 2
DEEP, LOW = 8, 4
ROWS_DEV = 4
SLOTS = 4
UNROLL = 16
LANES = 128


def env_place():
    return lax.axis_index("z") * LOW + lax.axis_index("y_lo")


def split(row):
    return row >> 5, row >> 3 & 3, row >> 2 & 1, row & 3


def read_place(row):
    half_at, x_at, _ = (lax.axis_index(a) for a in GRP)
    y, x, core, rest = split(row)
    return (x_at - x & 3) << 4 | core << 3 | (y ^ half_at) << 2 | rest


def write_place(row):
    half_at, x_at, core_at = (lax.axis_index(a) for a in GRP)
    y, x, core, rest = split(row)
    y = y ^ half_at
    x = jnp.where(y == 0, x - x_at & 3, x)
    return (core ^ core_at) << 5 | y << 4 | x << 2 | rest


def word_of(slot, index, row, block):
    return slot | index << 7 | row << 12 | block << 19


def parts_of(word):
    return word & 127, word >> 7 & 31, word >> 12 & 127, word >> 19


def pack_kernel(
    per,
    sector,
    column,
    source,
    target,
    index,
    sector_rows,
    tiles,
    out_1,
    out_2,
    out_3,
    out_4,
    need,
    picked,
    heads,
    nexts,
    counts,
    started,
    copies,
):
    place = env_place()
    columns = column.shape[0]
    sectors = heads.shape[0]

    rows = sector_rows[...]
    lane = lax.broadcasted_iota(jnp.int32, rows.shape, 1) % per
    rank = jnp.ones(rows.shape, jnp.int32)
    for step in range(1, per):
        same = (pltpu.roll(rows, step, 1) == rows) & (lane >= step)
        rank = rank + same.astype(jnp.int32)
    wanted = rows == column[0]
    for c in range(1, columns):
        wanted = wanted | (rows == column[c])
    slots = jnp.maximum(jnp.max(jnp.where(wanted, rank, 0)), 1)
    need[0] = slots

    def clear(s, carry):
        heads[s] = -1
        counts[s] = 0
        return carry

    lax.fori_loop(0, sectors, clear, 0, unroll=8)

    def chain(c, carry):
        s = column[c]
        nexts[c] = heads[s]
        heads[s] = c
        return carry

    lax.fori_loop(0, columns, chain, 0, unroll=8)

    outs = (out_1, out_2, out_3, out_4)

    def move(i, out, slot, place):
        return pltpu.make_async_copy(tiles.at[i], out.at[place], copies.at[slot])

    def tile(i, n):
        s = sector[place * per + i]
        k = counts[s]
        counts[s] = k + 1

        def send(state):
            c, n = state
            slot = c * slots + k
            for size in range(1, SLOTS + 1):

                @pl.when(slots == size)
                def _(size=size):
                    move(i, outs[size - 1], slot, slot).start()

            started[n] = slot
            return nexts[c], n + 1

        return lax.while_loop(lambda state: state[0] >= 0, send, (heads[s], n))[1]

    sent = lax.fori_loop(0, per, tile, jnp.int32(0))

    mine = column[place]

    def scan(b, n):
        k = b * slots
        for i in range(per):
            t = b * per + i
            match = (sector[t] == mine).astype(jnp.int32)
            picked[n] = t * LANES + k
            n = n + match
            k = k + match
        return n

    n = lax.fori_loop(0, sector.shape[0] // per, scan, jnp.int32(1))
    spare = HALVES * XS * CORES * ROWS_DEV
    for j in range(UNROLL):
        picked[n + j] = word_of(0, 0, spare, 0)
    picked[0] = n - 1

    def resolve(j, carry):
        t = picked[j] >> 7
        row, block = write_place(target[t]), read_place(source[t])
        picked[j] = word_of(picked[j] & 127, index[t], row, block)
        return carry

    lax.fori_loop(1, n, resolve, 0)

    def finish(j, carry):
        move(0, out_1, started[j], 0).wait()
        return carry

    lax.fori_loop(0, sent, finish, 0)


def apply_kernel(
    picked,
    need,
    tiles,
    part_0,
    part_1,
    part_2,
    part_3,
    rights,
    out_stay,
    out_cross,
    out_other_stay,
    out_other_cross,
    held,
    acc,
    blocks,
    copied,
):
    size = tiles.shape[0] // SLOTS

    def load_slot(slot):
        at = pl.ds(slot * size, size)
        return pltpu.make_async_copy(tiles.at[at], held.at[at], copied.at[XS + slot])

    for slot in range(SLOTS):

        @pl.when(need[0] > slot)
        def _(slot=slot):
            load_slot(slot).start()

    loads = []
    for x, part in enumerate((part_0, part_1, part_2, part_3)):
        at = blocks.at[pl.ds(x * part.shape[0], part.shape[0])]
        loads.append(pltpu.make_async_copy(part, at, copied.at[x]))
    for load in loads:
        load.start()
    quarter = out_stay.shape[0]
    count = 4 * quarter

    def clear(r, carry):
        acc[r] = jnp.zeros(acc.shape[1:], acc.dtype)
        return carry

    lax.fori_loop(0, count, clear, 0, unroll=4)
    for load in loads:
        load.wait()

    def arrive(slot, carry):
        load_slot(slot).wait()
        return carry

    def terms(j, here):
        last = picked[jnp.minimum((j + 1) * UNROLL, picked[0])]
        wanted = lax.div(parts_of(last)[0], jnp.int32(size)) + 1
        lax.fori_loop(here, wanted, arrive, 0)
        words = [parts_of(picked[1 + j * UNROLL + u]) for u in range(UNROLL)]
        products = [
            jnp.dot(
                held[slot], blocks[block], preferred_element_type=jnp.float32
            ).astype(jnp.bfloat16)
            for slot, _, _, block in words
        ]
        images = [
            jnp.dot(product, rights[tile], preferred_element_type=jnp.float32)
            for product, (_, tile, _, _) in zip(products, words)
        ]
        for (_, _, row, _), image in zip(words, images):
            acc[row] += image
        return jnp.maximum(here, wanted)

    here = lax.fori_loop(
        0, (picked[0] + UNROLL - 1) // UNROLL, terms, jnp.int32(0)
    )
    lax.fori_loop(here, need[0], arrive, 0)

    def finish(r, carry):
        for place, out in enumerate(
            (out_stay, out_cross, out_other_stay, out_other_cross)
        ):
            out[r] = acc[place * quarter + r].astype(out.dtype)
        return carry

    lax.fori_loop(0, quarter, finish, 0)


def place_kernel(got, out, copied):
    move = pltpu.make_async_copy(got, out.at[pl.ds(0, got.shape[0])], copied)
    move.start()
    move.wait()


def swap(value, axis):
    return lax.ppermute(value, axis, [(0, 1), (1, 0)])


def add(left, right):
    total = left.astype(jnp.float32) + right.astype(jnp.float32)
    return total.astype(jnp.bfloat16)


def step_x(value, step):
    return lax.ppermute(value, "x", [(i, (i + step) % XS) for i in range(XS)])


def exchange(slots, packing):
    def run(*packed):
        got = lax.all_to_all(packed[slots - 1], ENV, 0, 0, tiled=True)
        if slots == SLOTS:
            return got
        return pl.pallas_call(
            place_kernel,
            out_shape=packing,
            in_specs=[pl.BlockSpec(memory_space=pltpu.VMEM)],
            out_specs=pl.BlockSpec(memory_space=pl.ANY),
            scratch_shapes=[pltpu.SemaphoreType.DMA],
        )(got)

    return run


def shards(
    wavefunction,
    left_tiles,
    right_tiles,
    term_source,
    term_target,
    right_index,
    term_sector,
    column_sector,
):
    per, size, _ = left_tiles.shape
    columns = column_sector.shape[0]
    smem = pl.BlockSpec(memory_space=pltpu.SMEM)
    vmem = pl.BlockSpec(memory_space=pltpu.VMEM)
    anywhere = pl.BlockSpec(memory_space=pl.ANY)
    sectors = term_sector[:, 0]
    slots = columns * SLOTS
    packing = jax.ShapeDtypeStruct((slots, size, size), jnp.bfloat16)

    psi = wavefunction.reshape(-1, size, size)
    across = swap(psi, "y_hi")
    *packed, need, picked = pl.pallas_call(
        lambda *refs: pack_kernel(per, *refs),
        out_shape=(
            *[
                jax.ShapeDtypeStruct((columns * (k + 1), size, size), jnp.bfloat16)
                for k in range(SLOTS)
            ],
            jax.ShapeDtypeStruct((1,), jnp.int32),
            jax.ShapeDtypeStruct((sectors.shape[0] + 1 + UNROLL,), jnp.int32),
        ),
        in_specs=[smem] * 5 + [vmem] * 2,
        out_specs=(*[anywhere] * SLOTS, smem, smem),
        scratch_shapes=[pltpu.SMEM((columns,), jnp.int32)] * 3
        + [pltpu.SMEM((slots,), jnp.int32), pltpu.SemaphoreType.DMA((slots,))],
        cost_estimate=pl.CostEstimate(
            flops=0, bytes_accessed=8 * 2**20, transcendentals=0
        ),
    )(
        sectors,
        column_sector,
        term_source,
        term_target,
        right_index,
        sectors.reshape(-1, LANES),
        left_tiles,
    )
    packed, across = lax.optimization_barrier((packed, across))
    pair = jnp.concatenate([psi, across])
    quad = lax.all_gather(pair, "core", axis=0, tiled=True)
    parts = [quad] + [step_x(quad, step) for step in range(1, XS)]
    tiles = lax.switch(
        need[0] - 1, [exchange(k + 1, packing) for k in range(SLOTS)], *packed
    )
    tiles, parts = lax.optimization_barrier((tiles, parts))
    quarter = quad.shape[0]
    block = jax.ShapeDtypeStruct(quad.shape, jnp.bfloat16)
    stay, cross, other_stay, other_cross = pl.pallas_call(
        apply_kernel,
        out_shape=[block] * 4,
        in_specs=[smem] * 2 + [anywhere] * (1 + XS) + [vmem],
        out_specs=[vmem] * 4,
        scratch_shapes=[
            pltpu.VMEM(packing.shape, jnp.bfloat16),
            pltpu.VMEM((4 * quarter + 1, size, size), jnp.float32),
            pltpu.VMEM((4 * quarter, size, size), jnp.bfloat16),
            pltpu.SemaphoreType.DMA((SLOTS + XS,)),
        ],
        compiler_params=pltpu.CompilerParams(vmem_limit_bytes=40 * 2**20),
    )(
        picked,
        need,
        tiles,
        *parts,
        right_tiles,
    )
    cross = add(cross, swap(other_cross, "core"))
    cross = lax.all_to_all(cross, "x", 0, 0, tiled=True)
    cross = jnp.sum(cross.reshape((XS,) + psi.shape).astype(jnp.float32), axis=0)
    cross = cross.astype(jnp.bfloat16)
    stay = add(stay, swap(other_stay, "core")).reshape((XS,) + psi.shape)
    *early, last = stay
    cross, last = lax.optimization_barrier((cross, last))
    crossed = swap(cross, "y_hi")
    total = early[0].astype(jnp.float32) + crossed.astype(jnp.float32)
    for step, value in enumerate([*early[1:], last], 1):
        total = total + step_x(value, step).astype(jnp.float32)
    return total.astype(jnp.bfloat16).reshape(wavefunction.shape)


def solution(mesh):
    physical = Mesh(mesh.devices.reshape(HALVES, XS, CORES, DEEP, LOW), GRP + ENV)
    placed = (
        P(GRP, ENV),
        P(GRP + ENV, None, None),
        P(None, ENV, None),
        P(GRP),
        P(GRP),
        P(GRP),
        P(GRP, None),
        P(),
    )
    return jax.shard_map(
        shards, mesh=physical, in_specs=placed, out_specs=P(GRP, ENV), check_vma=False
    )
```

```python
import jax
import jax.numpy as jnp
from jax import lax
from jax.experimental import pallas as pl
from jax.experimental.pallas import tpu as pltpu
from jax.sharding import Mesh
from jax.sharding import PartitionSpec as P

GRP = ("y_hi", "x", "core")
ENV = ("z", "y_lo")
HALVES, XS, CORES = 2, 4, 2
DEEP, LOW = 8, 4
ROWS_DEV = 4
SLOTS = 4
UNROLL = 16
LANES = 128


def env_place():
    return lax.axis_index("z") * LOW + lax.axis_index("y_lo")


def split(row):
    return row >> 5, row >> 3 & 3, row >> 2 & 1, row & 3


def read_place(row):
    half_at, x_at, _ = (lax.axis_index(a) for a in GRP)
    y, x, core, rest = split(row)
    return (x_at - x & 3) << 4 | core << 3 | (y ^ half_at) << 2 | rest


def write_place(row):
    half_at, x_at, core_at = (lax.axis_index(a) for a in GRP)
    y, x, core, rest = split(row)
    y = y ^ half_at
    x = jnp.where(y == 0, x - x_at & 3, x)
    return (core ^ core_at) << 5 | y << 4 | x << 2 | rest


def word_of(slot, index, row, block):
    return slot | index << 7 | row << 12 | block << 19


def parts_of(word):
    return word & 127, word >> 7 & 31, word >> 12 & 127, word >> 19


def pack_kernel(
    per,
    sector,
    column,
    source,
    target,
    index,
    sector_rows,
    tiles,
    out_1,
    out_2,
    out_3,
    out_4,
    need,
    picked,
    heads,
    nexts,
    counts,
    started,
    copies,
):
    place = env_place()
    columns = column.shape[0]
    sectors = heads.shape[0]

    rows = sector_rows[...]
    lane = lax.broadcasted_iota(jnp.int32, rows.shape, 1) % per
    rank = jnp.ones(rows.shape, jnp.int32)
    for step in range(1, per):
        same = (pltpu.roll(rows, step, 1) == rows) & (lane >= step)
        rank = rank + same.astype(jnp.int32)
    wanted = rows == column[0]
    for c in range(1, columns):
        wanted = wanted | (rows == column[c])
    slots = jnp.maximum(jnp.max(jnp.where(wanted, rank, 0)), 1)
    need[0] = slots

    def clear(s, carry):
        heads[s] = -1
        counts[s] = 0
        return carry

    lax.fori_loop(0, sectors, clear, 0, unroll=8)

    def chain(c, carry):
        s = column[c]
        nexts[c] = heads[s]
        heads[s] = c
        return carry

    lax.fori_loop(0, columns, chain, 0, unroll=8)

    outs = (out_1, out_2, out_3, out_4)

    def move(i, out, slot, place):
        return pltpu.make_async_copy(tiles.at[i], out.at[place], copies.at[slot])

    def tile(i, n):
        s = sector[place * per + i]
        k = counts[s]
        counts[s] = k + 1

        def send(state):
            c, n = state
            slot = c * slots + k
            for size in range(1, SLOTS + 1):

                @pl.when(slots == size)
                def _(size=size):
                    move(i, outs[size - 1], slot, slot).start()

            started[n] = slot
            return nexts[c], n + 1

        return lax.while_loop(lambda state: state[0] >= 0, send, (heads[s], n))[1]

    sent = lax.fori_loop(0, per, tile, jnp.int32(0))

    mine = column[place]

    def scan(b, n):
        k = b * slots
        for i in range(per):
            t = b * per + i
            match = (sector[t] == mine).astype(jnp.int32)
            picked[n] = t * LANES + k
            n = n + match
            k = k + match
        return n

    n = lax.fori_loop(0, sector.shape[0] // per, scan, jnp.int32(1))
    spare = HALVES * XS * CORES * ROWS_DEV
    for j in range(UNROLL):
        picked[n + j] = word_of(0, 0, spare, 0)
    picked[0] = n - 1

    def resolve(j, carry):
        t = picked[j] >> 7
        row, block = write_place(target[t]), read_place(source[t])
        picked[j] = word_of(picked[j] & 127, index[t], row, block)
        return carry

    lax.fori_loop(1, n, resolve, 0)

    def finish(j, carry):
        move(0, out_1, started[j], 0).wait()
        return carry

    lax.fori_loop(0, sent, finish, 0)


def apply_kernel(
    picked,
    need,
    tiles_1,
    tiles_2,
    tiles_3,
    tiles_4,
    part_0,
    part_1,
    part_2,
    part_3,
    rights,
    out_stay,
    out_cross,
    out_other_stay,
    out_other_cross,
    held,
    acc,
    blocks,
    copied,
):
    size = tiles_1.shape[0]

    def load_slot(tiles, place, slot):
        source = tiles.at[pl.ds(place * size, size)]
        held_at = held.at[pl.ds(slot * size, size)]
        return pltpu.make_async_copy(source, held_at, copied.at[XS + slot])

    for slots, tiles in enumerate((tiles_1, tiles_2, tiles_3, tiles_4), 1):

        @pl.when(need[0] == slots)
        def _(slots=slots, tiles=tiles):
            for slot in range(slots):
                load_slot(tiles, slot, slot).start()

    loads = []
    for x, part in enumerate((part_0, part_1, part_2, part_3)):
        at = blocks.at[pl.ds(x * part.shape[0], part.shape[0])]
        loads.append(pltpu.make_async_copy(part, at, copied.at[x]))
    for load in loads:
        load.start()
    quarter = out_stay.shape[0]
    count = 4 * quarter

    def clear(r, carry):
        acc[r] = jnp.zeros(acc.shape[1:], acc.dtype)
        return carry

    lax.fori_loop(0, count, clear, 0, unroll=4)
    for load in loads:
        load.wait()

    def arrive(slot, carry):
        load_slot(tiles_1, 0, slot).wait()
        return carry

    def terms(j, here):
        last = picked[jnp.minimum((j + 1) * UNROLL, picked[0])]
        wanted = lax.div(parts_of(last)[0], jnp.int32(size)) + 1
        lax.fori_loop(here, wanted, arrive, 0)
        words = [parts_of(picked[1 + j * UNROLL + u]) for u in range(UNROLL)]
        products = [
            jnp.dot(
                held[slot], blocks[block], preferred_element_type=jnp.float32
            ).astype(jnp.bfloat16)
            for slot, _, _, block in words
        ]
        images = [
            jnp.dot(product, rights[tile], preferred_element_type=jnp.float32)
            for product, (_, tile, _, _) in zip(products, words)
        ]
        for (_, _, row, _), image in zip(words, images):
            acc[row] += image
        return jnp.maximum(here, wanted)

    here = lax.fori_loop(
        0, (picked[0] + UNROLL - 1) // UNROLL, terms, jnp.int32(0)
    )
    lax.fori_loop(here, need[0], arrive, 0)

    def finish(r, carry):
        for place, out in enumerate(
            (out_stay, out_cross, out_other_stay, out_other_cross)
        ):
            out[r] = acc[place * quarter + r].astype(out.dtype)
        return carry

    lax.fori_loop(0, quarter, finish, 0)


def blank_kernel(*outs):
    pass


def swap(value, axis):
    return lax.ppermute(value, axis, [(0, 1), (1, 0)])


def add(left, right):
    total = left.astype(jnp.float32) + right.astype(jnp.float32)
    return total.astype(jnp.bfloat16)


def step_x(value, step):
    return lax.ppermute(value, "x", [(i, (i + step) % XS) for i in range(XS)])


def exchange(slots):
    def run(*packed):
        got = lax.all_to_all(packed[slots - 1], ENV, 0, 0, tiled=True)
        others = [p for k, p in enumerate(packed) if k != slots - 1]
        blanks = pl.pallas_call(
            blank_kernel,
            out_shape=[jax.ShapeDtypeStruct(p.shape, p.dtype) for p in others],
            out_specs=[pl.BlockSpec(memory_space=pl.ANY)] * len(others),
        )()
        return (*blanks[: slots - 1], got, *blanks[slots - 1 :])

    return run


def shards(
    wavefunction,
    left_tiles,
    right_tiles,
    term_source,
    term_target,
    right_index,
    term_sector,
    column_sector,
):
    per, size, _ = left_tiles.shape
    columns = column_sector.shape[0]
    smem = pl.BlockSpec(memory_space=pltpu.SMEM)
    vmem = pl.BlockSpec(memory_space=pltpu.VMEM)
    anywhere = pl.BlockSpec(memory_space=pl.ANY)
    sectors = term_sector[:, 0]
    slots = columns * SLOTS
    packing = jax.ShapeDtypeStruct((slots, size, size), jnp.bfloat16)

    psi = wavefunction.reshape(-1, size, size)
    across = swap(psi, "y_hi")
    *packed, need, picked = pl.pallas_call(
        lambda *refs: pack_kernel(per, *refs),
        out_shape=(
            *[
                jax.ShapeDtypeStruct((columns * (k + 1), size, size), jnp.bfloat16)
                for k in range(SLOTS)
            ],
            jax.ShapeDtypeStruct((1,), jnp.int32),
            jax.ShapeDtypeStruct((sectors.shape[0] + 1 + UNROLL,), jnp.int32),
        ),
        in_specs=[smem] * 5 + [vmem] * 2,
        out_specs=(*[anywhere] * SLOTS, smem, smem),
        scratch_shapes=[pltpu.SMEM((columns,), jnp.int32)] * 3
        + [pltpu.SMEM((slots,), jnp.int32), pltpu.SemaphoreType.DMA((slots,))],
        cost_estimate=pl.CostEstimate(
            flops=0, bytes_accessed=8 * 2**20, transcendentals=0
        ),
    )(
        sectors,
        column_sector,
        term_source,
        term_target,
        right_index,
        sectors.reshape(-1, LANES),
        left_tiles,
    )
    packed, across = lax.optimization_barrier((packed, across))
    pair = jnp.concatenate([psi, across])
    quad = lax.all_gather(pair, "core", axis=0, tiled=True)
    parts = [quad] + [step_x(quad, step) for step in range(1, XS)]
    tiles = lax.switch(
        need[0] - 1, [exchange(k + 1) for k in range(SLOTS)], *packed
    )
    tiles, parts = lax.optimization_barrier((tiles, parts))
    quarter = quad.shape[0]
    block = jax.ShapeDtypeStruct(quad.shape, jnp.bfloat16)
    stay, cross, other_stay, other_cross = pl.pallas_call(
        apply_kernel,
        out_shape=[block] * 4,
        in_specs=[smem] * 2 + [anywhere] * (SLOTS + XS) + [vmem],
        out_specs=[vmem] * 4,
        scratch_shapes=[
            pltpu.VMEM(packing.shape, jnp.bfloat16),
            pltpu.VMEM((4 * quarter + 1, size, size), jnp.float32),
            pltpu.VMEM((4 * quarter, size, size), jnp.bfloat16),
            pltpu.SemaphoreType.DMA((SLOTS + XS,)),
        ],
        compiler_params=pltpu.CompilerParams(vmem_limit_bytes=40 * 2**20),
    )(
        picked,
        need,
        *tiles,
        *parts,
        right_tiles,
    )
    cross = add(cross, swap(other_cross, "core"))
    cross = lax.all_to_all(cross, "x", 0, 0, tiled=True)
    cross = jnp.sum(cross.reshape((XS,) + psi.shape).astype(jnp.float32), axis=0)
    cross = cross.astype(jnp.bfloat16)
    stay = add(stay, swap(other_stay, "core")).reshape((XS,) + psi.shape)
    *early, last = stay
    cross, last = lax.optimization_barrier((cross, last))
    crossed = swap(cross, "y_hi")
    total = early[0].astype(jnp.float32) + crossed.astype(jnp.float32)
    for step, value in enumerate([*early[1:], last], 1):
        total = total + step_x(value, step).astype(jnp.float32)
    return total.astype(jnp.bfloat16).reshape(wavefunction.shape)


def solution(mesh):
    physical = Mesh(mesh.devices.reshape(HALVES, XS, CORES, DEEP, LOW), GRP + ENV)
    placed = (
        P(GRP, ENV),
        P(GRP + ENV, None, None),
        P(None, ENV, None),
        P(GRP),
        P(GRP),
        P(GRP),
        P(GRP, None),
        P(),
    )
    return jax.shard_map(
        shards, mesh=physical, in_specs=placed, out_specs=P(GRP, ENV), check_vma=False
    )
```
